128 devices in a mesh: ctx: 8 (over z, x_hi), exp: 16 (over y, x_lo, core).
Axes of the slice: x: 4 (x_hi: 2, x_lo: 2; x = x_hi * 2 + x_lo), y: 4, z: 4, core: 2. Of those that a mesh axis runs over, the one named last changes fastest.
Arguments:
- query_rows: bfloat16 [16, 1024, 5120], P('exp', 'ctx'), may hold values from -5 to 5
- key_rows: bfloat16 [16, 1024, 1024], P('exp', 'ctx'), may hold values from -5 to 5
- value_rows: bfloat16 [16, 1024, 1024], P('exp', 'ctx'), may hold values from -6 to 6
- stream: bfloat16 [16, 1024, 5120], P('exp', 'ctx'), may hold values from -33 to 33
- out_grad: bfloat16 [16, 1024, 5120], P('exp', 'ctx'), may hold values from -6 to 6
- route_weight: float32 [16, 1024], P('exp', 'ctx'), may hold values from 0.2 to 1
- expert_ids: int32 [16, 1024, 1], P('exp', 'ctx'), may hold values from 0 to 15
- span_order: int32 [16], replicated, may hold values from 0 to 15, each once
- norm_gain: float32 [5120], replicated, may hold values from 0.1 to 1.9
- expert_gate: bfloat16 [16, 5120, 4096], P('exp', None, 'ctx'), may hold values from -0.078125 to 0.078125
- expert_in: bfloat16 [16, 5120, 4096], P('exp', None, 'ctx'), may hold values from -0.078125 to 0.078125
- expert_out: bfloat16 [16, 4096, 5120], P('exp', 'ctx'), may hold values from -0.09375 to 0.09375
Outputs:
- grad_stream: bfloat16 [16, 1024, 5120], P('exp', 'ctx')
- grad_query: bfloat16 [16, 1024, 5120], P('exp', 'ctx')
- grad_key: bfloat16 [16, 1024, 1024], P('exp', 'ctx')
- grad_value: bfloat16 [16, 1024, 1024], P('exp', 'ctx')
The draws below stay inside these ranges and needn't reach their ends.
All inputs are finite; a program needn't handle non-finite values.
Results may differ from the reference program's by a relative error of at most 0.039.
Values may be sent and summed in bfloat16 or wider, within the bound.
No kernel may reach another device: no remote copies, remote signals or barrier semaphores. Data moves between devices by JAX's collectives and lax.ppermute only.
A program may use at most 192 MiB of HBM per device.

```python
import math
import jax
import jax.numpy as jnp
from jax import lax

D = 5120
H = 40
KVH = 8
DH = 128
FF = 4096
TOK_DEV = 128
EXPERTS = 16
SEQS = 16
SEQ = 1024
SPAN = 64
CAP = 4
N_CTX = 8
N_EXP = 16


def draw_query_rows(key, part):
    key = jax.random.fold_in(key, 11)
    shape_here = (SEQS, SEQ, KVH, H // KVH, DH)
    result_rows = jnp.clip(jax.random.normal(key, shape_here), -4.0, 4.0)
    return result_rows.reshape(SEQS, SEQ, H * DH).astype(jnp.bfloat16)


def draw_key_rows(key, part):
    key = jax.random.fold_in(key, 12)
    shape_here = (SEQS, SEQ, KVH, DH)
    result_rows = jnp.clip(jax.random.normal(key, shape_here), -4.0, 4.0)
    return result_rows.reshape(SEQS, SEQ, KVH * DH).astype(jnp.bfloat16)


def draw_stream(key, part):
    key = jax.random.fold_in(key, 13)
    row_key, col_key, value_key = jax.random.split(key, 3)
    row_scale = jnp.exp(jax.random.uniform(row_key, (SEQS, SEQ, 1), minval=math.log(0.3), maxval=math.log(3.0)))
    col_scale = jnp.exp(jax.random.uniform(col_key, (1, 1, D), minval=-1.0, maxval=1.0))
    values = jnp.clip(jax.random.normal(value_key, (SEQS, SEQ, D)), -4.0, 4.0)
    return (values * row_scale * col_scale).astype(jnp.bfloat16)


def block_scale(rng, extent, cuts, low, high):
    loudness = 1.0
    for dim, parts in cuts:
        heights = jax.random.uniform(jax.random.fold_in(jax.random.fold_in(rng, 6), dim), (parts,), jnp.float32, low / len(cuts), high / len(cuts))
        loudness = loudness * jnp.repeat(jnp.exp(heights), extent[dim] // parts).reshape((-1,) + (1,) * (len(extent) - 1 - dim))
    return loudness


def choose_distinct(rng, rows, count, top, lift):
    order = jax.random.permutation(jax.random.fold_in(rng, 1), count)
    favour = order
    for power in range(3):
        favour = favour * favour // count
    favour = favour * lift // count
    tickets = jax.random.randint(jax.random.fold_in(rng, 2), (rows, count), 0, 4096) + favour
    fixed_rows = jax.random.permutation(jax.random.fold_in(rng, 3), rows)[jnp.arange(count) % rows]
    tickets = jnp.where(jnp.arange(rows)[:, None] == fixed_rows[None, :], 1 << 14, tickets)
    score = tickets * count + jnp.arange(count)
    return lax.top_k(score.astype(jnp.int32), top)[1].astype(jnp.int32)


def gaussian(rng, dims, spread, most, shards=(), held_as=jnp.bfloat16):
    array = spread * jax.random.normal(rng, dims, jnp.float32)
    if shards:
        array = array * block_scale(rng, dims, shards, -0.22, 0.18)
    return jnp.clip(array, -most, most).astype(held_as)


def setup_inputs(seed: int = 0) -> dict:
    streams_of = jax.random.split(jax.random.key(seed), 13)
    return {
        "query_rows": draw_query_rows(jax.random.fold_in(streams_of[12], 71), 0),
        "key_rows": draw_key_rows(jax.random.fold_in(streams_of[12], 71), 0),
        "value_rows": gaussian(streams_of[2], (SEQS, SEQ, KVH * DH), 1.0, 6.0, ((0, 16), (1, 8))),
        "stream": draw_stream(jax.random.fold_in(streams_of[12], 71), 0),
        "out_grad": gaussian(streams_of[4], (SEQS, SEQ, D), 1.0, 6.0, ((0, 16), (1, 8))),
        "route_weight": jnp.clip(0.2 + 0.8 * jax.random.uniform(streams_of[5], (SEQS, SEQ), jnp.float32) ** block_scale(streams_of[5], (SEQS, SEQ), ((0, 16), (1, 8)), -0.2, 0.2), 0.2, 1.0),
        "expert_ids": choose_distinct(streams_of[6], SEQS * SEQ, EXPERTS, 1, 1024).reshape((SEQS, SEQ, 1)),
        "span_order": jax.random.permutation(streams_of[7], 2 * N_CTX).astype(jnp.int32),
        "norm_gain": jnp.clip(1.0 + 0.18 * jax.random.normal(streams_of[8], (D,), jnp.float32), 0.1, 1.9),
        "expert_gate": gaussian(streams_of[9], (EXPERTS, D, FF), D ** -0.5, 0.078125, ((0, 16), (2, 8))),
        "expert_in": gaussian(streams_of[10], (EXPERTS, D, FF), D ** -0.5, 0.078125, ((0, 16), (2, 8))),
        "expert_out": gaussian(streams_of[11], (EXPERTS, FF, D), FF ** -0.5, 0.09375, ((0, 16), (1, 8))),
    }


EPSILON = 1e-05

def normalize(stream_f, norm_gain):
    return stream_f * lax.rsqrt(lax.optimization_barrier(jnp.mean(stream_f * stream_f, axis=-1, keepdims=True)) + EPSILON) * norm_gain.astype(jnp.float32)

def rounded(values):
    return lax.optimization_barrier(values.astype(jnp.bfloat16)).astype(jnp.float32)

def stored_positions(span_order):
    storage = jnp.arange(SEQ, dtype=jnp.int32)
    return jnp.take(span_order, storage // SPAN).astype(jnp.int32) * SPAN + storage % SPAN

def attend_block(query_b, keys_all, values_all, grad_b, query_pos, key_pos):
    group_size = H // KVH
    factor = DH ** (-0.5)
    queries = query_b.reshape(-1, KVH, group_size, DH).astype(jnp.float32)
    grad_heads = grad_b.reshape(-1, KVH, group_size, DH).astype(jnp.float32)
    keys_f = keys_all.reshape(-1, KVH, DH).astype(jnp.float32)
    values_f = values_all.reshape(-1, KVH, DH).astype(jnp.float32)
    scores = jnp.einsum('tkgd,skd->kgts', queries, keys_f) * factor
    visible = key_pos[None, :] <= query_pos[:, None]
    scores = jnp.where(visible, scores, -1e+30)
    row_peak = lax.optimization_barrier(jnp.max(scores, axis=-1, keepdims=True))
    weights = jnp.exp(scores - row_peak)
    attn_probs = weights / lax.optimization_barrier(jnp.sum(weights, axis=-1, keepdims=True))
    probs_b = rounded(attn_probs)
    attended = jnp.einsum('kgts,skd->tkgd', probs_b, values_f)
    row_delta = lax.optimization_barrier(jnp.sum(grad_heads * attended, axis=-1))
    dprobs = jnp.einsum('tkgd,skd->kgts', grad_heads, values_f)
    dscores = rounded(attn_probs * (dprobs - jnp.transpose(row_delta, (1, 2, 0))[..., None]))
    grad_q = jnp.einsum('kgts,skd->tkgd', dscores, keys_f) * factor
    key_part = jnp.einsum('kgts,tkgd->skd', dscores, queries) * factor
    value_part = jnp.einsum('kgts,tkgd->skd', probs_b, grad_heads)
    return (grad_q.reshape(query_b.shape).astype(jnp.bfloat16), key_part.reshape(keys_all.shape), value_part.reshape(values_all.shape))

def reference(query_rows, key_rows, value_rows, stream, out_grad, route_weight, expert_ids, span_order, norm_gain, expert_gate, expert_in, expert_out):
    stream_f = stream.reshape(-1, D).astype(jnp.float32)
    normed = normalize(stream_f, norm_gain)
    normed_b = normed.astype(jnp.bfloat16)
    routed_b = (out_grad.reshape(-1, D).astype(jnp.float32) * route_weight.reshape(-1, 1)).astype(jnp.bfloat16)
    expert_flat = expert_ids.reshape(-1).astype(jnp.int32)
    blocked = expert_flat.reshape(-1, TOK_DEV)
    onehot = (blocked[:, :, None] == jnp.arange(EXPERTS, dtype=jnp.int32)[None, None, :]).astype(jnp.int32)
    slot_rank = lax.optimization_barrier(jnp.sum((jnp.cumsum(onehot, axis=1) - 1) * onehot, axis=2)).reshape(-1)
    kept_rows = slot_rank < CAP
    slot_total = N_CTX * N_EXP * CAP
    shard_width = FF // N_CTX

    def expert_step(expert_at, running):
        w_gate_one = lax.dynamic_index_in_dim(expert_gate, expert_at, 0, keepdims=False)
        w_in_one = lax.dynamic_index_in_dim(expert_in, expert_at, 0, keepdims=False)
        w_out_one = lax.dynamic_index_in_dim(expert_out, expert_at, 0, keepdims=False)
        chosen = kept_rows & (expert_flat == expert_at)
        rows_at = jnp.nonzero(chosen, size=slot_total, fill_value=0)[0]
        live_rows = (jnp.arange(slot_total, dtype=jnp.int32) < jnp.sum(chosen.astype(jnp.int32))).astype(jnp.float32)[:, None]
        inputs = normed_b[rows_at]
        cotangent = routed_b[rows_at]
        gate_pre = jnp.dot(inputs, w_gate_one, preferred_element_type=jnp.float32)
        up_pre = jnp.dot(inputs, w_in_one, preferred_element_type=jnp.float32)
        backed = jnp.dot(cotangent, w_out_one.T, preferred_element_type=jnp.float32)
        gate_sig = jax.nn.sigmoid(gate_pre)
        grad_gate = (backed * up_pre * gate_sig * (1.0 + gate_pre * (1.0 - gate_sig))).astype(jnp.bfloat16)
        grad_up = (backed * gate_pre * gate_sig).astype(jnp.bfloat16)
        summed = jnp.zeros((slot_total, D), jnp.float32)
        for shard_at in range(N_CTX):
            first_col = shard_at * shard_width
            last_col = first_col + shard_width
            block_term = jnp.dot(grad_gate[:, first_col:last_col], w_gate_one[:, first_col:last_col].T, preferred_element_type=jnp.float32)
            block_term = block_term + jnp.dot(grad_up[:, first_col:last_col], w_in_one[:, first_col:last_col].T, preferred_element_type=jnp.float32)
            summed = summed + rounded(block_term)
        return running.at[rows_at].add(summed * live_rows)
    input_grad = lax.fori_loop(0, EXPERTS, expert_step, jnp.zeros((stream_f.shape[0], D), jnp.float32))

    def normed_of(values):
        return normalize(values, norm_gain)
    _, pullback = jax.vjp(normed_of, stream_f)
    stream_grad = pullback(input_grad)[0]
    grad_total = (out_grad.reshape(-1, D).astype(jnp.float32) + stream_grad).astype(jnp.bfloat16)
    grad_stream = grad_total.reshape(SEQS, SEQ, D)
    key_pos = stored_positions(span_order)

    def attend_sequence(operands):
        query_seq, key_seq, value_seq, grad_seq = operands
        key_total = jnp.zeros(key_seq.shape, jnp.float32)
        value_total = jnp.zeros(value_seq.shape, jnp.float32)
        grad_blocks = []
        for shard_at in range(N_CTX):
            row_start = shard_at * TOK_DEV
            grad_q, key_part, value_part = attend_block(query_seq[row_start:row_start + TOK_DEV], key_seq, value_seq, grad_seq[row_start:row_start + TOK_DEV], key_pos[row_start:row_start + TOK_DEV], key_pos)
            grad_blocks.append(grad_q)
            key_total = key_total + rounded(key_part)
            value_total = value_total + rounded(value_part)
        return (jnp.concatenate(grad_blocks, axis=0), key_total.astype(jnp.bfloat16), value_total.astype(jnp.bfloat16))
    grad_query, grad_key, grad_value = lax.map(attend_sequence, (query_rows, key_rows, value_rows, grad_stream))
    return (grad_stream, grad_query, grad_key, grad_value)
```

```python
import functools

import jax
import jax.numpy as jnp
from jax import lax
from jax.experimental import pallas as pl
from jax.experimental.pallas import tpu as pltpu
from jax.sharding import PartitionSpec as P

D = 5120
H = 40
KVH = 8
DH = 128
GROUP = H // KVH
EXPERTS = 16
CAP = 4
TOK = 128
SEQ = 1024
SPAN = 64
SPANS = SEQ // SPAN
FFD = 512
EPSILON = 1e-05
F32 = jnp.float32
BF16 = jnp.bfloat16
QB = 256
NQ = SEQ // QB
GW = GROUP * DH
IN_CHUNKS = 2
OUT_CHUNKS = 2
DI = D // IN_CHUNKS
DO = D // OUT_CHUNKS
KB = 512
SHIFTS = (1, 3, 2)
FACTOR = DH ** (-0.5)


def nn(a, b):
    return lax.dot_general(a, b, (((1,), (0,)), ((), ())), preferred_element_type=F32)


def nt(a, b):
    return lax.dot_general(a, b, (((1,), (1,)), ((), ())), preferred_element_type=F32)


def tn(a, b):
    return lax.dot_general(a, b, (((0,), (0,)), ((), ())), preferred_element_type=F32)


def iota(shape, dim):
    return lax.broadcasted_iota(jnp.int32, shape, dim)


def params(mb=48):
    return pltpu.CompilerParams(vmem_limit_bytes=mb * 1024 * 1024)


def sds(shape, dtype=BF16):
    return jax.ShapeDtypeStruct(shape, dtype)


VM = pl.BlockSpec(memory_space=pltpu.VMEM)


def dispatch_kernel(stream, out_grad, weight, ids, gain, *outs):
    rows, picks = outs[:-1], outs[-1]
    onehot = ids[...] == iota((TOK, 128), 1)
    onehot_f = onehot.astype(F32)
    lower = (iota((TOK, TOK), 1) < iota((TOK, TOK), 0)).astype(BF16)
    before = nn(lower, onehot_f.astype(BF16))
    rank = jnp.sum(before * onehot_f, axis=1, keepdims=True).astype(jnp.int32)
    lane = iota((TOK, 128), 1)
    target = ids[...] * 8 + rank
    kept = rank < CAP
    pick_n = ((lane == target) & kept).astype(BF16)
    pick_r = ((lane == target + CAP) & kept).astype(BF16)
    pick = jnp.concatenate([pick_n, pick_r], axis=0)
    picks[...] = pick
    total = jnp.zeros((TOK, 1), F32)
    for at in range(0, D, 640):
        part = stream[:, at:at + 640].astype(F32)
        total = total + jnp.sum(part * part, axis=1, keepdims=True)
    scale = lax.rsqrt(total / D + EPSILON)
    for chunk in range(IN_CHUNKS):
        for at in range(0, DI, 640):
            cols = slice(chunk * DI + at, chunk * DI + at + 640)
            normed = stream[:, cols].astype(F32) * scale * gain[:, cols]
            routed = out_grad[:, cols].astype(F32) * weight[...]
            both = jnp.concatenate([normed.astype(BF16), routed.astype(BF16)], axis=0)
            rows[chunk][:, at:at + 640] = tn(pick, both).astype(BF16)


def dispatch(stream, out_grad, weight, ids, gain):
    return pl.pallas_call(
        dispatch_kernel,
        out_shape=[sds((TOK, DI))] * IN_CHUNKS + [sds((2 * TOK, 128))],
        in_specs=[VM] * 5,
        out_specs=[VM] * (IN_CHUNKS + 1),
        compiler_params=params(),
        name="dispatch",
    )(stream, out_grad, weight, ids, gain)


def split_rows():
    out = iota((128, 128), 0)
    inn = iota((128, 128), 1)
    want = ((out >> 5) & 1) * 64 + ((out >> 2) & 7) * 8 + (out >> 6) * 4 + (out & 3)
    return (inn == want).astype(BF16)


def project_kernel(first, last, counts, *refs):
    n_pieces = len(counts)
    pieces = refs[:n_pieces]
    w_gate, w_in, w_out = refs[n_pieces:n_pieces + 3]
    rest = refs[n_pieces + 3:]
    if not first:
        carried, rest = rest[:3], rest[3:]
    if last:
        outs, rest = rest[:2], rest[2:]
    else:
        outs, rest = rest[:3], rest[3:]
    x_at, r_at, gate, up, backed = rest
    step = pl.program_id(0)

    @pl.when(step == 0)
    def _():
        if first:
            gate[...] = jnp.zeros_like(gate)
            up[...] = jnp.zeros_like(up)
            backed[...] = jnp.zeros_like(backed)
        else:
            gate[...] = carried[0][...]
            up[...] = carried[1][...]
            backed[...] = carried[2][...]

    mover = split_rows()
    groups = []
    for ref, count in zip(pieces, counts):
        for at in range(count):
            groups.append(ref[at * 64:(at + 1) * 64, :])
    for at in range(0, len(groups), 2):
        moved = nn(mover, jnp.concatenate(groups[at:at + 2], axis=0)).astype(BF16)
        x_at[at * 32:at * 32 + 64, :] = moved[:64]
        r_at[at * 32:at * 32 + 64, :] = moved[64:]
    gate[...] += nn(x_at[...], w_gate[0])
    up[...] += nn(x_at[...], w_in[0])
    backed[...] += nt(r_at[...], w_out[0])

    @pl.when(step == pl.num_programs(0) - 1)
    def _():
        if last:
            sig = jax.nn.sigmoid(gate[...])
            outs[0][...] = (
                backed[...] * up[...] * sig * (1.0 + gate[...] * (1.0 - sig))
            ).astype(BF16)
            outs[1][...] = (backed[...] * gate[...] * sig).astype(BF16)
        else:
            outs[0][...] = gate[...]
            outs[1][...] = up[...]
            outs[2][...] = backed[...]


def project(chunk, pieces, carried, w_gate, w_in, w_out):
    first, last = chunk == 0, chunk == IN_CHUNKS - 1
    counts = tuple(p.shape[0] // 64 for p in pieces)
    base = chunk * (DI // KB)
    rows = sum(counts) * 32
    whole = pl.BlockSpec((rows, FFD), lambda i: (0, 0))
    in_specs = [pl.BlockSpec((p.shape[0], KB), lambda i: (0, i)) for p in pieces]
    in_specs += [
        pl.BlockSpec((1, KB, FFD), lambda i: (0, base + i, 0)),
        pl.BlockSpec((1, KB, FFD), lambda i: (0, base + i, 0)),
        pl.BlockSpec((1, FFD, KB), lambda i: (0, 0, base + i)),
    ]
    in_specs += [whole] * len(carried)
    outs = [sds((rows, FFD))] * 2 if last else [sds((rows, FFD), F32)] * 3
    return pl.pallas_call(
        functools.partial(project_kernel, first, last, counts),
        grid=(DI // KB,),
        out_shape=outs,
        in_specs=in_specs,
        out_specs=[whole] * len(outs),
        scratch_shapes=[pltpu.VMEM((rows, KB), BF16)] * 2 + [pltpu.VMEM((rows, FFD), F32)] * 3,
        compiler_params=params(),
        cost_estimate=pl.CostEstimate(
            flops=6 * rows * DI * FFD, bytes_accessed=30 * 1024 * 1024 // IN_CHUNKS, transcendentals=0
        ),
        name="project",
    )(*pieces, w_gate, w_in, w_out, *carried)


TERM_ROWS = (64, 64, 64, 64, 128, 128)


def term_kernel(grad_gate, grad_up, w_gate, w_in, *outs):
    block = nt(grad_gate[...], w_gate[0]) + nt(grad_up[...], w_in[0])
    block = block.astype(BF16)
    at = 0
    for ref, rows in zip(outs, TERM_ROWS):
        ref[...] = block[at:at + rows]
        at += rows


def terms(chunk, grad_gate, grad_up, w_gate, w_in):
    base = chunk * (DO // KB)
    whole = pl.BlockSpec(grad_gate.shape, lambda i: (0, 0))
    weight = pl.BlockSpec((1, KB, FFD), lambda i: (0, base + i, 0))
    return pl.pallas_call(
        term_kernel,
        grid=(DO // KB,),
        out_shape=[sds((r, DO)) for r in TERM_ROWS],
        in_specs=[whole, whole, weight, weight],
        out_specs=[pl.BlockSpec((r, KB), lambda i: (0, i)) for r in TERM_ROWS],
        compiler_params=params(),
        cost_estimate=pl.CostEstimate(
            flops=4 * 512 * DO * FFD, bytes_accessed=16 * 1024 * 1024 // OUT_CHUNKS, transcendentals=0
        ),
        name="terms",
    )(grad_gate, grad_up, w_gate, w_in)


def settle_kernel(a_own, a_swap, b_own, b1, b3, b2, out):
    half = DO // 2
    a = a_own[...] + a_swap[...].astype(F32)
    b = b_own[...] + b1[...].astype(F32) + b3[...].astype(F32) + b2[...].astype(F32)
    both = jnp.concatenate([a, b], axis=0).astype(BF16)
    stacked = jnp.concatenate([both[:, :half], both[:, half:]], axis=0)
    o = iota((128, 128), 0)
    want = ((o >> 2) & 1) * 64 + (o >> 3) * 4 + (o & 3)
    mover = (iota((128, 128), 1) == want).astype(BF16)
    out[...] = nn(mover, stacked).astype(BF16)


def settle(*args):
    return pl.pallas_call(
        settle_kernel,
        out_shape=sds((128, DO // 2)),
        in_specs=[VM] * 6,
        out_specs=VM,
        compiler_params=params(),
        name="settle",
    )(*args)


def finish_kernel(stream, out_grad, gain, picks, *refs):
    parts, (grad, grad_cut, scaled) = refs[:OUT_CHUNKS], refs[OUT_CHUNKS:]
    half = DO // 2
    square = jnp.zeros((TOK, 1), F32)
    dots = jnp.zeros((TOK, 1), F32)
    for chunk in range(OUT_CHUNKS):
        for at in range(0, half, 640):
            got = nn(picks[...], parts[chunk][:, at:at + 640])
            for side in range(2):
                cols = slice(chunk * DO + side * half + at, chunk * DO + side * half + at + 640)
                x = stream[:, cols].astype(F32)
                u = got[side * TOK:(side + 1) * TOK] * gain[:, cols]
                square = square + jnp.sum(x * x, axis=1, keepdims=True)
                dots = dots + jnp.sum(x * u, axis=1, keepdims=True)
                scaled[:, cols] = u
    r = lax.rsqrt(square / D + EPSILON)
    coef = dots * (r * r * r) / D
    for group in range(KVH):
        cols = slice(group * GW, (group + 1) * GW)
        x = stream[:, cols].astype(F32)
        total = out_grad[:, cols].astype(F32) + (scaled[:, cols] * r - x * coef)
        total = total.astype(BF16)
        grad[:, cols] = total
        grad_cut[group] = total


def finish(stream, out_grad, gain, picks, parts):
    return pl.pallas_call(
        finish_kernel,
        out_shape=[sds((TOK, D)), sds((KVH, TOK, GW))],
        in_specs=[VM] * (4 + len(parts)),
        out_specs=[VM] * 2,
        scratch_shapes=[pltpu.VMEM((TOK, D), F32)],
        compiler_params=params(),
        name="finish",
    )(stream, out_grad, gain, picks, *parts)


def probs_kernel(order, rows, probs, q_out, kv_out, q_at, kv_at):
    head = pl.program_id(0)

    @pl.when(head == 0)
    def _():
        for s in range(SPANS):
            to = pl.ds(pl.multiple_of(order[s] * SPAN, SPAN), SPAN)
            block = rows[s * SPAN:(s + 1) * SPAN, :]
            for g in range(GROUP):
                q_at[g, to, :] = block[:, g * DH:(g + 1) * DH]
            kv_at[0, to, :] = block[:, GW:GW + DH]
            kv_at[1, to, :] = block[:, GW + DH:GW + 2 * DH]
        q_out[...] = q_at[...]
        kv_out[...] = kv_at[...]

    for i in range(NQ):
        n = QB * (i + 1)
        q = q_at[head, i * QB:n, :]
        scores = nt(kv_at[0, 0:n, :], q) * FACTOR
        visible = iota((n, QB), 0) <= iota((n, QB), 1) + i * QB
        scores = jnp.where(visible, scores, -1e30)
        peak = jnp.max(scores, axis=0, keepdims=True)
        weights = jnp.exp(scores - peak)
        weights = weights / jnp.sum(weights, axis=0, keepdims=True)
        probs[0, i, 0:n, :] = weights.astype(BF16)


def make_probs(order, rows):
    return pl.pallas_call(
        probs_kernel,
        grid_spec=pltpu.PrefetchScalarGridSpec(
            num_scalar_prefetch=1,
            grid=(GROUP,),
            in_specs=[pl.BlockSpec((SEQ, GW + 2 * DH), lambda h, o: (0, 0))],
            out_specs=[
                pl.BlockSpec((1, NQ, SEQ, QB), lambda h, o: (h, 0, 0, 0)),
                pl.BlockSpec((GROUP, SEQ, DH), lambda h, o: (0, 0, 0)),
                pl.BlockSpec((2, SEQ, DH), lambda h, o: (0, 0, 0)),
            ],
            scratch_shapes=[
                pltpu.VMEM((GROUP, SEQ, DH), BF16),
                pltpu.VMEM((2, SEQ, DH), BF16),
            ],
        ),
        out_shape=[
            sds((GROUP, NQ, SEQ, QB)),
            sds((GROUP, SEQ, DH)),
            sds((2, SEQ, DH)),
        ],
        compiler_params=params(),
        cost_estimate=pl.CostEstimate(
            flops=2 * GROUP * SEQ * SEQ * DH, bytes_accessed=14 * 1024 * 1024, transcendentals=GROUP * SEQ * SEQ
        ),
        name="probs",
    )(order, rows)


def attend_kernel(order, probs, q, kv, grads, out, g_at, kt_at, dq_at, dk_at, dv_at):
    head = pl.program_id(0)

    @pl.when(head == 0)
    def _():
        for s in range(SPANS):
            to = pl.ds(pl.multiple_of(order[s] * SPAN, SPAN), SPAN)
            block = grads[s * SPAN:(s + 1) * SPAN, :]
            for g in range(GROUP):
                g_at[g, to, :] = block[:, g * DH:(g + 1) * DH]
        kt_at[...] = kv[0].T
        dk_at[...] = jnp.zeros_like(dk_at)
        dv_at[...] = jnp.zeros_like(dv_at)

    for i in range(NQ):
        n = QB * (i + 1)
        g_i = g_at[head, i * QB:n, :]
        q_i = q[head, i * QB:n, :]
        p_b = probs[0, i, 0:n, :]
        p = p_b.astype(F32)
        dp = nt(kv[1, 0:n, :], g_i)
        delta = jnp.sum(p * dp, axis=0, keepdims=True)
        ds = (p * (dp - delta)).astype(BF16)
        dv_at[0:n, :] += nn(p_b, g_i)
        dk_at[0:n, :] += nn(ds, q_i)
        dq_at[i * QB:n, :] = (nn(kt_at[:, 0:n], ds) * FACTOR).T.astype(BF16)
    for s in range(SPANS):
        at = pl.ds(pl.multiple_of(order[s] * SPAN, SPAN), SPAN)
        to = slice(s * SPAN, (s + 1) * SPAN)
        out[to, pl.ds(pl.multiple_of(head * DH, DH), DH)] = dq_at[at, :]

    @pl.when(head == GROUP - 1)
    def _():
        for s in range(SPANS):
            at = pl.ds(pl.multiple_of(order[s] * SPAN, SPAN), SPAN)
            to = slice(s * SPAN, (s + 1) * SPAN)
            out[to, GW:GW + DH] = (dk_at[at, :] * FACTOR).astype(BF16)
            out[to, GW + DH:GW + 2 * DH] = dv_at[at, :].astype(BF16)


def attend(order, probs, q, kv, grads):
    return pl.pallas_call(
        attend_kernel,
        grid_spec=pltpu.PrefetchScalarGridSpec(
            num_scalar_prefetch=1,
            grid=(GROUP,),
            in_specs=[
                pl.BlockSpec((1, NQ, SEQ, QB), lambda h, o: (h, 0, 0, 0)),
                pl.BlockSpec((GROUP, SEQ, DH), lambda h, o: (0, 0, 0)),
                pl.BlockSpec((2, SEQ, DH), lambda h, o: (0, 0, 0)),
                pl.BlockSpec((SEQ, GW), lambda h, o: (0, 0)),
            ],
            out_specs=pl.BlockSpec((SEQ, GW + 2 * DH), lambda h, o: (0, 0)),
            scratch_shapes=[
                pltpu.VMEM((GROUP, SEQ, DH), BF16),
                pltpu.VMEM((DH, SEQ), BF16),
                pltpu.VMEM((SEQ, DH), BF16),
                pltpu.VMEM((SEQ, DH), F32),
                pltpu.VMEM((SEQ, DH), F32),
            ],
        ),
        out_shape=sds((SEQ, GW + 2 * DH)),
        compiler_params=params(),
        cost_estimate=pl.CostEstimate(
            flops=8 * GROUP * SEQ * SEQ * DH, bytes_accessed=16 * 1024 * 1024, transcendentals=0
        ),
        name="attend",
    )(order, probs, q, kv, grads)


def along_z(x, shift):
    pairs = [(c, ((c // 2 + shift) % 4) * 2 + c % 2) for c in range(8)]
    return lax.ppermute(x, "ctx", pairs)


def across_x(x):
    return lax.ppermute(x, "ctx", [(c, c ^ 1) for c in range(8)])


def gather_pieces(shard):
    a, b = shard[:64], shard[64:]
    a_x = across_x(a)
    b_z = [along_z(b, k) for k in SHIFTS]
    a_both = jnp.concatenate([a, a_x], axis=0)
    a_z = [along_z(a_both, k) for k in SHIFTS]
    b_x = [across_x(p) for p in [b] + b_z]
    return [a_both] + a_z + [b] + b_z + b_x


def scatter_sums(groups):
    a_own, b_own, b_far = groups[0], groups[4], groups[5]
    b_got = across_x(b_far)
    a_got = [along_z(g, -k) for g, k in zip(groups[1:4], SHIFTS)]
    b_sum = b_own.astype(F32) + b_got.astype(F32)
    b_low = b_sum.astype(BF16)
    b_back = [
        along_z(b_low[32 * (at + 1):32 * (at + 2)], -k) for at, k in enumerate(SHIFTS)
    ]
    a_sum = a_own.astype(F32)
    for got in a_got:
        a_sum = a_sum + got.astype(F32)
    a_swap = across_x(a_sum[32:].astype(BF16))
    return settle(a_sum[:32], a_swap, b_sum[:32], *b_back)


def swap_exp(x):
    return lax.all_to_all(x, "exp", split_axis=0, concat_axis=0, tiled=True)


def swap_ctx(x):
    return lax.all_to_all(x, "ctx", split_axis=0, concat_axis=0, tiled=True)


def body(
    query_rows,
    key_rows,
    value_rows,
    stream,
    out_grad,
    route_weight,
    expert_ids,
    span_order,
    norm_gain,
    expert_gate,
    expert_in,
    expert_out,
):
    gain = norm_gain.reshape(1, D)
    by_head = jnp.concatenate(
        [
            query_rows[0].reshape(TOK, KVH, GW),
            key_rows[0].reshape(TOK, KVH, DH),
            value_rows[0].reshape(TOK, KVH, DH),
        ],
        axis=2,
    ).transpose(1, 0, 2)
    *outgoing, picks = dispatch(
        stream[0], out_grad[0], route_weight.reshape(TOK, 1), expert_ids[0], gain
    )
    qkv = swap_ctx(by_head).reshape(SEQ, GW + 2 * DH)
    shards = [swap_exp(o.reshape(EXPERTS, 8, DI)).reshape(TOK, DI) for o in outgoing]
    probs, q_sorted, kv_sorted = make_probs(span_order, qkv)
    carried = []
    for chunk, shard in enumerate(shards):
        carried = project(
            chunk, gather_pieces(shard), carried, expert_gate, expert_in, expert_out
        )
    grad_gate, grad_up = carried
    parts = []
    for chunk in range(OUT_CHUNKS):
        settled = scatter_sums(terms(chunk, grad_gate, grad_up, expert_gate, expert_in))
        parts.append(swap_exp(settled.reshape(EXPERTS, 8, DO // 2)).reshape(TOK, DO // 2))
    grad_total, grad_cut = finish(stream[0], out_grad[0], gain, picks, parts)
    grads = swap_ctx(grad_cut).reshape(SEQ, GW)
    result = attend(span_order, probs, q_sorted, kv_sorted, grads)
    back = swap_ctx(result.reshape(KVH, TOK, GW + 2 * DH)).transpose(1, 0, 2)
    return (
        grad_total[None],
        back[:, :, :GW].reshape(1, TOK, D),
        back[:, :, GW:GW + DH].reshape(1, TOK, KVH * DH),
        back[:, :, GW + DH:].reshape(1, TOK, KVH * DH),
    )


def solution(mesh):
    rows = P("exp", "ctx", None)
    return jax.shard_map(
        body,
        mesh=mesh,
        in_specs=(
            rows,
            rows,
            rows,
            rows,
            rows,
            P("exp", "ctx"),
            rows,
            P(),
            P(),
            P("exp", None, "ctx"),
            P("exp", None, "ctx"),
            rows,
        ),
        out_specs=(rows, rows, rows, rows),
        check_vma=False,
    )
```

```python
import functools

import jax
import jax.numpy as jnp
from jax import lax
from jax.experimental import pallas as pl
from jax.experimental.pallas import tpu as pltpu
from jax.sharding import PartitionSpec as P

D = 5120
H = 40
KVH = 8
DH = 128
GROUP = H // KVH
EXPERTS = 16
CAP = 4
TOK = 128
SEQ = 1024
SPAN = 64
SPANS = SEQ // SPAN
FFD = 512
EPSILON = 1e-05
F32 = jnp.float32
BF16 = jnp.bfloat16
QB = 256
NQ = SEQ // QB
GW = GROUP * DH
HALF = D // 2
ROWS = 512
FIRST = 64
KB = 1024
TB = 1024
SHIFTS = (1, 3, 2)
FACTOR = DH ** (-0.5)


def nn(a, b):
    return lax.dot_general(a, b, (((1,), (0,)), ((), ())), preferred_element_type=F32)


def nt(a, b):
    return lax.dot_general(a, b, (((1,), (1,)), ((), ())), preferred_element_type=F32)


def tn(a, b):
    return lax.dot_general(a, b, (((0,), (0,)), ((), ())), preferred_element_type=F32)


def iota(shape, dim):
    return lax.broadcasted_iota(jnp.int32, shape, dim)


def params(mb=60):
    return pltpu.CompilerParams(vmem_limit_bytes=mb * 1024 * 1024)


def sds(shape, dtype=BF16):
    return jax.ShapeDtypeStruct(shape, dtype)


VM = pl.BlockSpec(memory_space=pltpu.VMEM)


def dispatch_kernel(stream, out_grad, weight, ids, gain, rows, picks):
    onehot = ids[...] == iota((TOK, 128), 1)
    onehot_f = onehot.astype(F32)
    lower = (iota((TOK, TOK), 1) < iota((TOK, TOK), 0)).astype(BF16)
    before = nn(lower, onehot_f.astype(BF16))
    rank = jnp.sum(before * onehot_f, axis=1, keepdims=True).astype(jnp.int32)
    lane = iota((TOK, 128), 1)
    target = ids[...] * 8 + rank
    kept = rank < CAP
    pick_n = ((lane == target) & kept).astype(BF16)
    pick_r = ((lane == target + CAP) & kept).astype(BF16)
    pick = jnp.concatenate([pick_n, pick_r], axis=0)
    picks[...] = pick
    total = jnp.zeros((TOK, 1), F32)
    for at in range(0, D, 640):
        part = stream[:, at:at + 640].astype(F32)
        total = total + jnp.sum(part * part, axis=1, keepdims=True)
    scale = lax.rsqrt(total / D + EPSILON)
    for at in range(0, D, 640):
        cols = slice(at, at + 640)
        normed = stream[:, cols].astype(F32) * scale * gain[:, cols]
        routed = out_grad[:, cols].astype(F32) * weight[...]
        both = jnp.concatenate([normed.astype(BF16), routed.astype(BF16)], axis=0)
        rows[:, cols] = tn(pick, both).astype(BF16)


def dispatch(stream, out_grad, weight, ids, gain):
    return pl.pallas_call(
        dispatch_kernel,
        out_shape=[sds((TOK, D)), sds((2 * TOK, 128))],
        in_specs=[VM] * 5,
        out_specs=[VM] * 2,
        compiler_params=params(24),
        name="dispatch",
    )(stream, out_grad, weight, ids, gain)


def sort_kernel(shard, *outs):
    out = iota((128, 128), 0)
    want = (out >> 6) * 64 + ((out >> 2) & 7) * 8 + ((out >> 5) & 1) * 4 + (out & 3)
    mover = (iota((128, 128), 1) == want).astype(BF16)
    for at in range(0, D, 1280):
        moved = nn(mover, shard[:, at:at + 1280]).astype(BF16)
        outs[0][:, at:at + 1280] = moved[:64]
        outs[1][:, at:at + 1280] = moved[64:]


def sort_rows(shard):
    return pl.pallas_call(
        sort_kernel,
        out_shape=[sds((64, D))] * 2,
        in_specs=[VM],
        out_specs=[VM] * 2,
        compiler_params=params(24),
        name="sort_rows",
    )(shard)


def project_kernel(*refs):
    tops = refs[:4]
    rests = refs[4:12]
    w_gate, w_in, w_out, grad_gate, grad_up, x_at, r_at, gate, up, backed = refs[12:]
    step = pl.program_id(0)

    @pl.when(step == 0)
    def _():
        gate[...] = jnp.zeros_like(gate)
        up[...] = jnp.zeros_like(up)
        backed[...] = jnp.zeros_like(backed)

    for at in range(8):
        top = tops[at // 2][(at % 2) * FIRST:(at % 2 + 1) * FIRST, :]
        low = rests[at]
        x_at[at * 64:at * 64 + 32, :] = top[:32]
        x_at[at * 64 + 32:at * 64 + 64, :] = low[:32]
        r_at[at * 64:at * 64 + 32, :] = top[32:]
        r_at[at * 64 + 32:at * 64 + 64, :] = low[32:]
    gate[...] += nn(x_at[...], w_gate[0])
    up[...] += nn(x_at[...], w_in[0])
    backed[...] += nt(r_at[...], w_out[0])

    @pl.when(step == pl.num_programs(0) - 1)
    def _():
        sig = jax.nn.sigmoid(gate[...])
        grad_gate[...] = (
            backed[...] * up[...] * sig * (1.0 + gate[...] * (1.0 - sig))
        ).astype(BF16)
        grad_up[...] = (backed[...] * gate[...] * sig).astype(BF16)


def project(pieces, w_gate, w_in, w_out):
    whole = pl.BlockSpec((ROWS, FFD), lambda i: (0, 0))
    in_specs = [pl.BlockSpec((p.shape[0], KB), lambda i: (0, i)) for p in pieces]
    in_specs += [
        pl.BlockSpec((1, KB, FFD), lambda i: (0, i, 0)),
        pl.BlockSpec((1, KB, FFD), lambda i: (0, i, 0)),
        pl.BlockSpec((1, FFD, KB), lambda i: (0, 0, i)),
    ]
    return pl.pallas_call(
        project_kernel,
        grid=(D // KB,),
        out_shape=[sds((ROWS, FFD))] * 2,
        in_specs=in_specs,
        out_specs=[whole] * 2,
        scratch_shapes=[pltpu.VMEM((ROWS, KB), BF16)] * 2
        + [pltpu.VMEM((ROWS, FFD), F32)] * 3,
        compiler_params=params(60),
        cost_estimate=pl.CostEstimate(
            flops=6 * ROWS * D * FFD, bytes_accessed=28 * 1024 * 1024, transcendentals=0
        ),
        name="project",
    )(*pieces, w_gate, w_in, w_out)


TERM_ROWS = (64, 64, 64, 64, 128, 128)


def term_kernel(grad_gate, grad_up, w_gate, w_in, *outs):
    block = nt(grad_gate[...], w_gate[0]) + nt(grad_up[...], w_in[0])
    block = block.astype(BF16)
    for k in range(4):
        for side in range(2):
            at = (2 * k + side) * 64
            outs[k][side * 32:(side + 1) * 32, :] = block[at:at + 32]
            outs[4 + side][k * 32:(k + 1) * 32, :] = block[at + 32:at + 64]


def terms(grad_gate, grad_up, w_gate, w_in):
    whole = pl.BlockSpec(grad_gate.shape, lambda i: (0, 0))
    weight = pl.BlockSpec((1, TB, FFD), lambda i: (0, i, 0))
    return pl.pallas_call(
        term_kernel,
        grid=(D // TB,),
        out_shape=[sds((r, D)) for r in TERM_ROWS],
        in_specs=[whole, whole, weight, weight],
        out_specs=[pl.BlockSpec((r, TB), lambda i: (0, i)) for r in TERM_ROWS],
        compiler_params=params(),
        cost_estimate=pl.CostEstimate(
            flops=4 * ROWS * D * FFD, bytes_accessed=16 * 1024 * 1024, transcendentals=0
        ),
        name="terms",
    )(grad_gate, grad_up, w_gate, w_in)


def settle_kernel(a_own, a_swap, b_own, b1, b3, b2, out):
    a = a_own[...] + a_swap[...].astype(F32)
    b = b_own[...] + b1[...].astype(F32) + b3[...].astype(F32) + b2[...].astype(F32)
    both = jnp.concatenate([a, b], axis=0).astype(BF16)
    stacked = jnp.concatenate([both[:, :HALF], both[:, HALF:]], axis=0)
    o = iota((128, 128), 0)
    want = ((o >> 2) & 1) * 64 + (o >> 3) * 4 + (o & 3)
    mover = (iota((128, 128), 1) == want).astype(BF16)
    out[...] = nn(mover, stacked).astype(BF16)


def settle(*args):
    return pl.pallas_call(
        settle_kernel,
        out_shape=sds((128, HALF)),
        in_specs=[VM] * 6,
        out_specs=VM,
        compiler_params=params(24),
        name="settle",
    )(*args)


def finish_kernel(stream, out_grad, gain, picks, part, grad, grad_cut, scaled):
    square = jnp.zeros((TOK, 1), F32)
    dots = jnp.zeros((TOK, 1), F32)
    for at in range(0, HALF, 640):
        got = nn(picks[...], part[:, at:at + 640])
        for half in range(2):
            cols = slice(half * HALF + at, half * HALF + at + 640)
            x = stream[:, cols].astype(F32)
            u = got[half * TOK:(half + 1) * TOK] * gain[:, cols]
            square = square + jnp.sum(x * x, axis=1, keepdims=True)
            dots = dots + jnp.sum(x * u, axis=1, keepdims=True)
            scaled[:, cols] = u
    r = lax.rsqrt(square / D + EPSILON)
    coef = dots * (r * r * r) / D
    for group in range(KVH):
        cols = slice(group * GW, (group + 1) * GW)
        x = stream[:, cols].astype(F32)
        total = out_grad[:, cols].astype(F32) + (scaled[:, cols] * r - x * coef)
        total = total.astype(BF16)
        grad[:, cols] = total
        grad_cut[group] = total


def finish(stream, out_grad, gain, picks, part):
    return pl.pallas_call(
        finish_kernel,
        out_shape=[sds((TOK, D)), sds((KVH, TOK, GW))],
        in_specs=[VM] * 5,
        out_specs=[VM] * 2,
        scratch_shapes=[pltpu.VMEM((TOK, D), F32)],
        compiler_params=params(24),
        name="finish",
    )(stream, out_grad, gain, picks, part)


def cut_kernel(q, k, v, out):
    for head in range(KVH):
        out[head, :, :GW] = q[:, head * GW:(head + 1) * GW]
        out[head, :, GW:GW + DH] = k[:, head * DH:(head + 1) * DH]
        out[head, :, GW + DH:] = v[:, head * DH:(head + 1) * DH]


def cut_heads(q, k, v):
    return pl.pallas_call(
        cut_kernel,
        out_shape=sds((KVH, TOK, GW + 2 * DH)),
        in_specs=[VM] * 3,
        out_specs=VM,
        compiler_params=params(),
        name="cut_heads",
    )(q, k, v)


def probs_kernel(order, rows, probs, attended, q_out, kv_out, q_at, kv_at, vt_at):
    head = pl.program_id(0)

    @pl.when(head == 0)
    def _():
        for s in range(SPANS):
            to = pl.ds(pl.multiple_of(order[s] * SPAN, SPAN), SPAN)
            block = rows[s * SPAN:(s + 1) * SPAN, :]
            for g in range(GROUP):
                q_at[g, to, :] = block[:, g * DH:(g + 1) * DH]
            kv_at[0, to, :] = block[:, GW:GW + DH]
            kv_at[1, to, :] = block[:, GW + DH:GW + 2 * DH]
        q_out[...] = q_at[...]
        kv_out[...] = kv_at[...]
        vt_at[...] = kv_at[1].T

    for i in range(NQ):
        n = QB * (i + 1)
        q = q_at[head, i * QB:n, :]
        scores = nt(kv_at[0, 0:n, :], q) * FACTOR
        visible = iota((n, QB), 0) <= iota((n, QB), 1) + i * QB
        scores = jnp.where(visible, scores, -1e30)
        peak = jnp.max(scores, axis=0, keepdims=True)
        weights = jnp.exp(scores - peak)
        weights = weights / jnp.sum(weights, axis=0, keepdims=True)
        weights_b = weights.astype(BF16)
        probs[0, i, 0:n, :] = weights_b
        attended[0, :, i * QB:n] = nn(vt_at[:, 0:n], weights_b)


def make_probs(order, rows):
    return pl.pallas_call(
        probs_kernel,
        grid_spec=pltpu.PrefetchScalarGridSpec(
            num_scalar_prefetch=1,
            grid=(GROUP,),
            in_specs=[pl.BlockSpec((SEQ, GW + 2 * DH), lambda h, o: (0, 0))],
            out_specs=[
                pl.BlockSpec((1, NQ, SEQ, QB), lambda h, o: (h, 0, 0, 0)),
                pl.BlockSpec((1, DH, SEQ), lambda h, o: (h, 0, 0)),
                pl.BlockSpec((GROUP, SEQ, DH), lambda h, o: (0, 0, 0)),
                pl.BlockSpec((2, SEQ, DH), lambda h, o: (0, 0, 0)),
            ],
            scratch_shapes=[
                pltpu.VMEM((GROUP, SEQ, DH), BF16),
                pltpu.VMEM((2, SEQ, DH), BF16),
                pltpu.VMEM((DH, SEQ), BF16),
            ],
        ),
        out_shape=[
            sds((GROUP, NQ, SEQ, QB)),
            sds((GROUP, DH, SEQ), F32),
            sds((GROUP, SEQ, DH)),
            sds((2, SEQ, DH)),
        ],
        compiler_params=params(),
        cost_estimate=pl.CostEstimate(
            flops=2 * GROUP * SEQ * SEQ * DH, bytes_accessed=14 * 1024 * 1024, transcendentals=GROUP * SEQ * SEQ
        ),
        name="probs",
    )(order, rows)


def attend_kernel(
    order, probs, attended, q, kv, grads, out, g_at, kt_at, dq_at, dk_at, dv_at
):
    head = pl.program_id(0)

    @pl.when(head == 0)
    def _():
        for s in range(SPANS):
            to = pl.ds(pl.multiple_of(order[s] * SPAN, SPAN), SPAN)
            block = grads[s * SPAN:(s + 1) * SPAN, :]
            for g in range(GROUP):
                g_at[g, to, :] = block[:, g * DH:(g + 1) * DH]
        kt_at[...] = kv[0].T
        dk_at[...] = jnp.zeros_like(dk_at)
        dv_at[...] = jnp.zeros_like(dv_at)

    g_t = g_at[head].T
    delta = jnp.sum(g_t.astype(F32) * attended[0], axis=0, keepdims=True)
    for i in range(NQ):
        n = QB * (i + 1)
        g_i = g_at[head, i * QB:n, :]
        q_i = q[head, i * QB:n, :]
        p_b = probs[0, i, 0:n, :]
        dp = nn(kv[1, 0:n, :], g_t[:, i * QB:n])
        ds = (p_b.astype(F32) * (dp - delta[:, i * QB:n])).astype(BF16)
        dv_at[0:n, :] += nn(p_b, g_i)
        dk_at[0:n, :] += nn(ds, q_i)
        dq_at[i * QB:n, :] = (nn(kt_at[:, 0:n], ds) * FACTOR).T.astype(BF16)
    for s in range(SPANS):
        at = pl.ds(pl.multiple_of(order[s] * SPAN, SPAN), SPAN)
        to = slice(s * SPAN, (s + 1) * SPAN)
        out[to, pl.ds(pl.multiple_of(head * DH, DH), DH)] = dq_at[at, :]

    @pl.when(head == GROUP - 1)
    def _():
        for s in range(SPANS):
            at = pl.ds(pl.multiple_of(order[s] * SPAN, SPAN), SPAN)
            to = slice(s * SPAN, (s + 1) * SPAN)
            out[to, GW:GW + DH] = (dk_at[at, :] * FACTOR).astype(BF16)
            out[to, GW + DH:GW + 2 * DH] = dv_at[at, :].astype(BF16)


def attend(order, probs, attended, q, kv, grads):
    return pl.pallas_call(
        attend_kernel,
        grid_spec=pltpu.PrefetchScalarGridSpec(
            num_scalar_prefetch=1,
            grid=(GROUP,),
            in_specs=[
                pl.BlockSpec((1, NQ, SEQ, QB), lambda h, o: (h, 0, 0, 0)),
                pl.BlockSpec((1, DH, SEQ), lambda h, o: (h, 0, 0)),
                pl.BlockSpec((GROUP, SEQ, DH), lambda h, o: (0, 0, 0)),
                pl.BlockSpec((2, SEQ, DH), lambda h, o: (0, 0, 0)),
                pl.BlockSpec((SEQ, GW), lambda h, o: (0, 0)),
            ],
            out_specs=pl.BlockSpec((SEQ, GW + 2 * DH), lambda h, o: (0, 0)),
            scratch_shapes=[
                pltpu.VMEM((GROUP, SEQ, DH), BF16),
                pltpu.VMEM((DH, SEQ), BF16),
                pltpu.VMEM((SEQ, DH), BF16),
                pltpu.VMEM((SEQ, DH), F32),
                pltpu.VMEM((SEQ, DH), F32),
            ],
        ),
        out_shape=sds((SEQ, GW + 2 * DH)),
        compiler_params=params(),
        cost_estimate=pl.CostEstimate(
            flops=8 * GROUP * SEQ * SEQ * DH, bytes_accessed=16 * 1024 * 1024, transcendentals=0
        ),
        name="attend",
    )(order, probs, attended, q, kv, grads)


def hold(x, *others):
    anywhere = pl.BlockSpec(memory_space=pl.ANY)
    return pl.pallas_call(
        lambda *refs: None,
        out_shape=sds(x.shape, x.dtype),
        in_specs=[anywhere] * (1 + len(others)),
        out_specs=anywhere,
        input_output_aliases={0: 0},
        name="hold",
    )(x, *others)


def along_z(x, shift):
    pairs = [(c, ((c // 2 + shift) % 4) * 2 + c % 2) for c in range(8)]
    return lax.ppermute(x, "ctx", pairs)


def across_x(x):
    return lax.ppermute(x, "ctx", [(c, c ^ 1) for c in range(8)])


def gather_pieces(shard):
    a, b = sort_rows(shard)
    a_x = across_x(a)
    b_z = [along_z(b, k) for k in SHIFTS]
    a_both = jnp.concatenate([a, a_x], axis=0)
    a_z = [along_z(a_both, k) for k in SHIFTS]
    rests = []
    for p in [b] + b_z:
        rests += [p, across_x(p)]
    return [a_both] + a_z + rests


def scatter_sums(groups, tie):
    a_own, b_own, b_far = groups[0], groups[4], groups[5]
    b_got = across_x(hold(b_far, tie))
    a_got = [along_z(g, -k) for g, k in zip(groups[1:4], SHIFTS)]
    b_sum = b_own.astype(F32) + b_got.astype(F32)
    b_low = b_sum.astype(BF16)
    b_back = [
        along_z(b_low[32 * (at + 1):32 * (at + 2)], -k) for at, k in enumerate(SHIFTS)
    ]
    a_sum = a_own.astype(F32)
    for got in a_got:
        a_sum = a_sum + got.astype(F32)
    a_swap = across_x(a_sum[32:].astype(BF16))
    return settle(a_sum[:32], a_swap, b_sum[:32], *b_back)


def swap_exp(x):
    return lax.all_to_all(x, "exp", split_axis=0, concat_axis=0, tiled=True)


def swap_ctx(x):
    return lax.all_to_all(x, "ctx", split_axis=0, concat_axis=0, tiled=True)


def body(
    query_rows,
    key_rows,
    value_rows,
    stream,
    out_grad,
    route_weight,
    expert_ids,
    span_order,
    norm_gain,
    expert_gate,
    expert_in,
    expert_out,
):
    gain = norm_gain.reshape(1, D)
    outgoing, picks = dispatch(
        stream[0], out_grad[0], route_weight.reshape(TOK, 1), expert_ids[0], gain
    )
    shard = swap_exp(outgoing.reshape(EXPERTS, 8, D)).reshape(TOK, D)
    pieces = gather_pieces(shard)
    by_head = hold(cut_heads(query_rows[0], key_rows[0], value_rows[0]), *pieces)
    qkv = swap_ctx(by_head).reshape(SEQ, GW + 2 * DH)
    grad_gate, grad_up = project(pieces, expert_gate, expert_in, expert_out)
    settled = scatter_sums(terms(grad_gate, grad_up, expert_gate, expert_in), qkv)
    part = swap_exp(settled.reshape(EXPERTS, 8, HALF)).reshape(TOK, HALF)
    probs, attended, q_sorted, kv_sorted = make_probs(span_order, qkv)
    grad_total, grad_cut = finish(stream[0], out_grad[0], gain, picks, part)
    grads = swap_ctx(grad_cut).reshape(SEQ, GW)
    result = attend(span_order, probs, attended, q_sorted, kv_sorted, grads)
    back = swap_ctx(result.reshape(KVH, TOK, GW + 2 * DH)).transpose(1, 0, 2)
    return (
        grad_total[None],
        back[:, :, :GW].reshape(1, TOK, D),
        back[:, :, GW:GW + DH].reshape(1, TOK, KVH * DH),
        back[:, :, GW + DH:].reshape(1, TOK, KVH * DH),
    )


def solution(mesh):
    rows = P("exp", "ctx", None)
    return jax.shard_map(
        body,
        mesh=mesh,
        in_specs=(
            rows,
            rows,
            rows,
            rows,
            rows,
            P("exp", "ctx"),
            rows,
            P(),
            P(),
            P("exp", None, "ctx"),
            P("exp", None, "ctx"),
            rows,
        ),
        out_specs=(rows, rows, rows, rows),
        check_vma=False,
    )
```

```python
import functools

import jax
import jax.numpy as jnp
from jax import lax
from jax.experimental import pallas as pl
from jax.experimental.pallas import tpu as pltpu
from jax.sharding import PartitionSpec as P

D = 5120
H = 40
KVH = 8
DH = 128
GROUP = H // KVH
EXPERTS = 16
CAP = 4
TOK = 128
SEQ = 1024
SPAN = 64
SPANS = SEQ // SPAN
FFD = 512
EPSILON = 1e-05
F32 = jnp.float32
BF16 = jnp.bfloat16
QB = 256
NQ = SEQ // QB
GW = GROUP * DH
HALF = D // 2
ROWS = 256
FIRST = 64
KB = 1024
TB = 1024
SHIFTS = (1, 3, 2)
FACTOR = DH ** (-0.5)


def nn(a, b):
    return lax.dot_general(a, b, (((1,), (0,)), ((), ())), preferred_element_type=F32)


def nt(a, b):
    return lax.dot_general(a, b, (((1,), (1,)), ((), ())), preferred_element_type=F32)


def tn(a, b):
    return lax.dot_general(a, b, (((0,), (0,)), ((), ())), preferred_element_type=F32)


def iota(shape, dim):
    return lax.broadcasted_iota(jnp.int32, shape, dim)


def params(mb=60):
    return pltpu.CompilerParams(vmem_limit_bytes=mb * 1024 * 1024)


def sds(shape, dtype=BF16):
    return jax.ShapeDtypeStruct(shape, dtype)


VM = pl.BlockSpec(memory_space=pltpu.VMEM)


def dispatch_kernel(stream, out_grad, weight, ids, gain, rows, picks):
    onehot = ids[...] == iota((TOK, 128), 1)
    onehot_f = onehot.astype(F32)
    lower = (iota((TOK, TOK), 1) < iota((TOK, TOK), 0)).astype(BF16)
    before = nn(lower, onehot_f.astype(BF16))
    rank = jnp.sum(before * onehot_f, axis=1, keepdims=True).astype(jnp.int32)
    lane = iota((TOK, 128), 1)
    target = ids[...] * 8 + rank
    kept = rank < CAP
    pick_n = ((lane == target) & kept).astype(BF16)
    pick_r = ((lane == target + CAP) & kept).astype(BF16)
    pick = jnp.concatenate([pick_n, pick_r], axis=0)
    picks[...] = pick
    total = jnp.zeros((TOK, 1), F32)
    for at in range(0, D, 640):
        part = stream[:, at:at + 640].astype(F32)
        total = total + jnp.sum(part * part, axis=1, keepdims=True)
    scale = lax.rsqrt(total / D + EPSILON)
    for at in range(0, D, 640):
        cols = slice(at, at + 640)
        normed = stream[:, cols].astype(F32) * scale * gain[:, cols]
        routed = out_grad[:, cols].astype(F32) * weight[...]
        both = jnp.concatenate([normed.astype(BF16), routed.astype(BF16)], axis=0)
        rows[:, cols] = tn(pick, both).astype(BF16)


def dispatch(stream, out_grad, weight, ids, gain):
    return pl.pallas_call(
        dispatch_kernel,
        out_shape=[sds((TOK, D)), sds((2 * TOK, 128))],
        in_specs=[VM] * 5,
        out_specs=[VM] * 2,
        compiler_params=params(24),
        name="dispatch",
    )(stream, out_grad, weight, ids, gain)


def sort_kernel(shard, *outs):
    out = iota((128, 128), 0)
    want = (out >> 6) * 64 + ((out >> 2) & 7) * 8 + ((out >> 5) & 1) * 4 + (out & 3)
    mover = (iota((128, 128), 1) == want).astype(BF16)
    for at in range(0, D, 1280):
        moved = nn(mover, shard[:, at:at + 1280]).astype(BF16)
        outs[0][:, at:at + 1280] = moved[:64]
        outs[1][:, at:at + 1280] = moved[64:]


def sort_rows(shard):
    return pl.pallas_call(
        sort_kernel,
        out_shape=[sds((64, D))] * 2,
        in_specs=[VM],
        out_specs=[VM] * 2,
        compiler_params=params(24),
        name="sort_rows",
    )(shard)


def project_kernel(n_pieces, *refs):
    pieces = refs[:n_pieces]
    w_gate, w_in, w_out, grad_gate, grad_up, x_at, r_at, gate, up, backed = refs[n_pieces:]
    step = pl.program_id(0)

    @pl.when(step == 0)
    def _():
        gate[...] = jnp.zeros_like(gate)
        up[...] = jnp.zeros_like(up)
        backed[...] = jnp.zeros_like(backed)

    at = 0
    for piece in pieces:
        for low in range(0, piece.shape[0], 64):
            x_at[at:at + 32, :] = piece[low:low + 32, :]
            r_at[at:at + 32, :] = piece[low + 32:low + 64, :]
            at += 32
    gate[...] += nn(x_at[...], w_gate[0])
    up[...] += nn(x_at[...], w_in[0])
    backed[...] += nt(r_at[...], w_out[0])

    @pl.when(step == pl.num_programs(0) - 1)
    def _():
        sig = jax.nn.sigmoid(gate[...])
        grad_gate[...] = (
            backed[...] * up[...] * sig * (1.0 + gate[...] * (1.0 - sig))
        ).astype(BF16)
        grad_up[...] = (backed[...] * gate[...] * sig).astype(BF16)


def project(pieces, w_gate, w_in, w_out):
    whole = pl.BlockSpec((ROWS, FFD), lambda i: (0, 0))
    in_specs = [pl.BlockSpec((p.shape[0], KB), lambda i: (0, i)) for p in pieces]
    in_specs += [
        pl.BlockSpec((1, KB, FFD), lambda i: (0, i, 0)),
        pl.BlockSpec((1, KB, FFD), lambda i: (0, i, 0)),
        pl.BlockSpec((1, FFD, KB), lambda i: (0, 0, i)),
    ]
    return pl.pallas_call(
        functools.partial(project_kernel, len(pieces)),
        grid=(D // KB,),
        out_shape=[sds((ROWS, FFD))] * 2,
        in_specs=in_specs,
        out_specs=[whole] * 2,
        scratch_shapes=[pltpu.VMEM((ROWS, KB), BF16)] * 2
        + [pltpu.VMEM((ROWS, FFD), F32)] * 3,
        compiler_params=params(60),
        cost_estimate=pl.CostEstimate(
            flops=6 * ROWS * D * FFD, bytes_accessed=28 * 1024 * 1024, transcendentals=0
        ),
        name="project",
    )(*pieces, w_gate, w_in, w_out)


def term_kernel(by_z, grad_gate, grad_up, w_gate, w_in, *outs):
    block = nt(grad_gate[...], w_gate[0]) + nt(grad_up[...], w_in[0])
    block = block.astype(BF16)
    for z in range(4):
        for side in range(2):
            rows = block[(2 * z + side) * 32:(2 * z + side + 1) * 32]
            if by_z:
                outs[z][side * 32:(side + 1) * 32, :] = rows
            else:
                outs[side][z * 32:(z + 1) * 32, :] = rows


def terms(by_z, grad_gate, grad_up, w_gate, w_in):
    whole = pl.BlockSpec(grad_gate.shape, lambda i: (0, 0))
    weight = pl.BlockSpec((1, TB, FFD), lambda i: (0, i, 0))
    sizes = (64,) * 4 if by_z else (128,) * 2
    return pl.pallas_call(
        functools.partial(term_kernel, by_z),
        grid=(D // TB,),
        out_shape=[sds((r, D)) for r in sizes],
        in_specs=[whole, whole, weight, weight],
        out_specs=[pl.BlockSpec((r, TB), lambda i: (0, i)) for r in sizes],
        compiler_params=params(60),
        cost_estimate=pl.CostEstimate(
            flops=4 * ROWS * D * FFD, bytes_accessed=14 * 1024 * 1024, transcendentals=0
        ),
        name="terms",
    )(grad_gate, grad_up, w_gate, w_in)


def settle_kernel(a_own, a_swap, b_own, b1, b3, b2, out):
    a = a_own[...] + a_swap[...].astype(F32)
    b = b_own[...] + b1[...].astype(F32) + b3[...].astype(F32) + b2[...].astype(F32)
    both = jnp.concatenate([a, b], axis=0).astype(BF16)
    stacked = jnp.concatenate([both[:, :HALF], both[:, HALF:]], axis=0)
    o = iota((128, 128), 0)
    want = ((o >> 2) & 1) * 64 + (o >> 3) * 4 + (o & 3)
    mover = (iota((128, 128), 1) == want).astype(BF16)
    out[...] = nn(mover, stacked).astype(BF16)


def settle(*args):
    return pl.pallas_call(
        settle_kernel,
        out_shape=sds((128, HALF)),
        in_specs=[VM] * 6,
        out_specs=VM,
        compiler_params=params(24),
        name="settle",
    )(*args)


def finish_kernel(stream, out_grad, gain, picks, part, grad, grad_cut, scaled):
    square = jnp.zeros((TOK, 1), F32)
    dots = jnp.zeros((TOK, 1), F32)
    for at in range(0, HALF, 640):
        got = nn(picks[...], part[:, at:at + 640])
        for half in range(2):
            cols = slice(half * HALF + at, half * HALF + at + 640)
            x = stream[:, cols].astype(F32)
            u = got[half * TOK:(half + 1) * TOK] * gain[:, cols]
            square = square + jnp.sum(x * x, axis=1, keepdims=True)
            dots = dots + jnp.sum(x * u, axis=1, keepdims=True)
            scaled[:, cols] = u
    r = lax.rsqrt(square / D + EPSILON)
    coef = dots * (r * r * r) / D
    for group in range(KVH):
        cols = slice(group * GW, (group + 1) * GW)
        x = stream[:, cols].astype(F32)
        total = out_grad[:, cols].astype(F32) + (scaled[:, cols] * r - x * coef)
        total = total.astype(BF16)
        grad[:, cols] = total
        grad_cut[group] = total


def finish(stream, out_grad, gain, picks, part):
    return pl.pallas_call(
        finish_kernel,
        out_shape=[sds((TOK, D)), sds((KVH, TOK, GW))],
        in_specs=[VM] * 5,
        out_specs=[VM] * 2,
        scratch_shapes=[pltpu.VMEM((TOK, D), F32)],
        compiler_params=params(24),
        name="finish",
    )(stream, out_grad, gain, picks, part)


def cut_kernel(q, k, v, out):
    for head in range(KVH):
        out[head, :, :GW] = q[:, head * GW:(head + 1) * GW]
        out[head, :, GW:GW + DH] = k[:, head * DH:(head + 1) * DH]
        out[head, :, GW + DH:] = v[:, head * DH:(head + 1) * DH]


def cut_heads(q, k, v):
    return pl.pallas_call(
        cut_kernel,
        out_shape=sds((KVH, TOK, GW + 2 * DH)),
        in_specs=[VM] * 3,
        out_specs=VM,
        compiler_params=params(),
        name="cut_heads",
    )(q, k, v)


def probs_kernel(order, rows, probs, attended, q_out, kv_out, q_at, kv_at, vt_at):
    head = pl.program_id(0)

    @pl.when(head == 0)
    def _():
        for s in range(SPANS):
            to = pl.ds(pl.multiple_of(order[s] * SPAN, SPAN), SPAN)
            block = rows[s * SPAN:(s + 1) * SPAN, :]
            for g in range(GROUP):
                q_at[g, to, :] = block[:, g * DH:(g + 1) * DH]
            kv_at[0, to, :] = block[:, GW:GW + DH]
            kv_at[1, to, :] = block[:, GW + DH:GW + 2 * DH]
        q_out[...] = q_at[...]
        kv_out[...] = kv_at[...]
        vt_at[...] = kv_at[1].T

    for i in range(NQ):
        n = QB * (i + 1)
        q = q_at[head, i * QB:n, :]
        scores = nt(kv_at[0, 0:n, :], q) * FACTOR
        visible = iota((n, QB), 0) <= iota((n, QB), 1) + i * QB
        scores = jnp.where(visible, scores, -1e30)
        peak = jnp.max(scores, axis=0, keepdims=True)
        weights = jnp.exp(scores - peak)
        weights = weights / jnp.sum(weights, axis=0, keepdims=True)
        weights_b = weights.astype(BF16)
        probs[0, i, 0:n, :] = weights_b
        attended[0, :, i * QB:n] = nn(vt_at[:, 0:n], weights_b)


def make_probs(order, rows):
    return pl.pallas_call(
        probs_kernel,
        grid_spec=pltpu.PrefetchScalarGridSpec(
            num_scalar_prefetch=1,
            grid=(GROUP,),
            in_specs=[pl.BlockSpec((SEQ, GW + 2 * DH), lambda h, o: (0, 0))],
            out_specs=[
                pl.BlockSpec((1, NQ, SEQ, QB), lambda h, o: (h, 0, 0, 0)),
                pl.BlockSpec((1, DH, SEQ), lambda h, o: (h, 0, 0)),
                pl.BlockSpec((GROUP, SEQ, DH), lambda h, o: (0, 0, 0)),
                pl.BlockSpec((2, SEQ, DH), lambda h, o: (0, 0, 0)),
            ],
            scratch_shapes=[
                pltpu.VMEM((GROUP, SEQ, DH), BF16),
                pltpu.VMEM((2, SEQ, DH), BF16),
                pltpu.VMEM((DH, SEQ), BF16),
            ],
        ),
        out_shape=[
            sds((GROUP, NQ, SEQ, QB)),
            sds((GROUP, DH, SEQ), F32),
            sds((GROUP, SEQ, DH)),
            sds((2, SEQ, DH)),
        ],
        compiler_params=params(),
        cost_estimate=pl.CostEstimate(
            flops=2 * GROUP * SEQ * SEQ * DH, bytes_accessed=14 * 1024 * 1024, transcendentals=GROUP * SEQ * SEQ
        ),
        name="probs",
    )(order, rows)


def attend_kernel(
    order, probs, attended, q, kv, grads, out, g_at, kt_at, dq_at, dk_at, dv_at
):
    head = pl.program_id(0)

    @pl.when(head == 0)
    def _():
        for s in range(SPANS):
            to = pl.ds(pl.multiple_of(order[s] * SPAN, SPAN), SPAN)
            block = grads[s * SPAN:(s + 1) * SPAN, :]
            for g in range(GROUP):
                g_at[g, to, :] = block[:, g * DH:(g + 1) * DH]
        kt_at[...] = kv[0].T
        dk_at[...] = jnp.zeros_like(dk_at)
        dv_at[...] = jnp.zeros_like(dv_at)

    g_t = g_at[head].T
    delta = jnp.sum(g_t.astype(F32) * attended[0], axis=0, keepdims=True)
    for i in range(NQ):
        n = QB * (i + 1)
        g_i = g_at[head, i * QB:n, :]
        q_i = q[head, i * QB:n, :]
        p_b = probs[0, i, 0:n, :]
        dp = nn(kv[1, 0:n, :], g_t[:, i * QB:n])
        ds = (p_b.astype(F32) * (dp - delta[:, i * QB:n])).astype(BF16)
        dv_at[0:n, :] += nn(p_b, g_i)
        dk_at[0:n, :] += nn(ds, q_i)
        dq_at[i * QB:n, :] = (nn(kt_at[:, 0:n], ds) * FACTOR).T.astype(BF16)
    for s in range(SPANS):
        at = pl.ds(pl.multiple_of(order[s] * SPAN, SPAN), SPAN)
        to = slice(s * SPAN, (s + 1) * SPAN)
        out[to, pl.ds(pl.multiple_of(head * DH, DH), DH)] = dq_at[at, :]

    @pl.when(head == GROUP - 1)
    def _():
        for s in range(SPANS):
            at = pl.ds(pl.multiple_of(order[s] * SPAN, SPAN), SPAN)
            to = slice(s * SPAN, (s + 1) * SPAN)
            out[to, GW:GW + DH] = (dk_at[at, :] * FACTOR).astype(BF16)
            out[to, GW + DH:GW + 2 * DH] = dv_at[at, :].astype(BF16)


def attend(order, probs, attended, q, kv, grads):
    return pl.pallas_call(
        attend_kernel,
        grid_spec=pltpu.PrefetchScalarGridSpec(
            num_scalar_prefetch=1,
            grid=(GROUP,),
            in_specs=[
                pl.BlockSpec((1, NQ, SEQ, QB), lambda h, o: (h, 0, 0, 0)),
                pl.BlockSpec((1, DH, SEQ), lambda h, o: (h, 0, 0)),
                pl.BlockSpec((GROUP, SEQ, DH), lambda h, o: (0, 0, 0)),
                pl.BlockSpec((2, SEQ, DH), lambda h, o: (0, 0, 0)),
                pl.BlockSpec((SEQ, GW), lambda h, o: (0, 0)),
            ],
            out_specs=pl.BlockSpec((SEQ, GW + 2 * DH), lambda h, o: (0, 0)),
            scratch_shapes=[
                pltpu.VMEM((GROUP, SEQ, DH), BF16),
                pltpu.VMEM((DH, SEQ), BF16),
                pltpu.VMEM((SEQ, DH), BF16),
                pltpu.VMEM((SEQ, DH), F32),
                pltpu.VMEM((SEQ, DH), F32),
            ],
        ),
        out_shape=sds((SEQ, GW + 2 * DH)),
        compiler_params=params(),
        cost_estimate=pl.CostEstimate(
            flops=8 * GROUP * SEQ * SEQ * DH, bytes_accessed=16 * 1024 * 1024, transcendentals=0
        ),
        name="attend",
    )(order, probs, attended, q, kv, grads)


def hold(x, *others):
    anywhere = pl.BlockSpec(memory_space=pl.ANY)
    return pl.pallas_call(
        lambda *refs: None,
        out_shape=sds(x.shape, x.dtype),
        in_specs=[anywhere] * (1 + len(others)),
        out_specs=anywhere,
        input_output_aliases={0: 0},
        name="hold",
    )(x, *others)


def place_kernel(block, dq, dk, dv):
    dq[...] = block[0, :, :GW]
    dk[...] = block[0, :, GW:GW + DH]
    dv[...] = block[0, :, GW + DH:]


def place(blocks):
    return pl.pallas_call(
        place_kernel,
        grid=(KVH,),
        out_shape=[sds((TOK, D)), sds((TOK, KVH * DH)), sds((TOK, KVH * DH))],
        in_specs=[pl.BlockSpec((1, TOK, GW + 2 * DH), lambda i: (i, 0, 0))],
        out_specs=[
            pl.BlockSpec((TOK, GW), lambda i: (0, i)),
            pl.BlockSpec((TOK, DH), lambda i: (0, i)),
            pl.BlockSpec((TOK, DH), lambda i: (0, i)),
        ],
        compiler_params=params(24),
        name="place",
    )(blocks)


def along_z(x, shift):
    pairs = [(c, ((c // 2 + shift) % 4) * 2 + c % 2) for c in range(8)]
    return lax.ppermute(x, "ctx", pairs)


def across_x(x):
    return lax.ppermute(x, "ctx", [(c, c ^ 1) for c in range(8)])


def gather_pieces(shard):
    a, b = sort_rows(shard)
    a_x = across_x(a)
    b_z = [along_z(b, k) for k in SHIFTS]
    a_both = jnp.concatenate([a, a_x], axis=0)
    a_z = [along_z(a_both, k) for k in SHIFTS]
    rests = []
    for p in [b] + b_z:
        rests += [p, across_x(p)]
    return [a_both] + a_z, rests


def scatter_sums(a_groups, b_groups, tie):
    a_own, (b_own, b_far) = a_groups[0], b_groups
    b_got = across_x(hold(b_far, tie))
    a_got = [along_z(g, -k) for g, k in zip(a_groups[1:], SHIFTS)]
    b_sum = b_own.astype(F32) + b_got.astype(F32)
    b_low = b_sum.astype(BF16)
    b_back = [
        along_z(b_low[32 * (at + 1):32 * (at + 2)], -k) for at, k in enumerate(SHIFTS)
    ]
    a_sum = a_own.astype(F32)
    for got in a_got:
        a_sum = a_sum + got.astype(F32)
    a_swap = across_x(a_sum[32:].astype(BF16))
    return settle(a_sum[:32], a_swap, b_sum[:32], *b_back)


def swap_exp(x):
    return lax.all_to_all(x, "exp", split_axis=0, concat_axis=0, tiled=True)


def swap_ctx(x):
    return lax.all_to_all(x, "ctx", split_axis=0, concat_axis=0, tiled=True)


def body(
    query_rows,
    key_rows,
    value_rows,
    stream,
    out_grad,
    route_weight,
    expert_ids,
    span_order,
    norm_gain,
    expert_gate,
    expert_in,
    expert_out,
):
    gain = norm_gain.reshape(1, D)
    outgoing, picks = dispatch(
        stream[0], out_grad[0], route_weight.reshape(TOK, 1), expert_ids[0], gain
    )
    shard = swap_exp(outgoing.reshape(EXPERTS, 8, D)).reshape(TOK, D)
    a_pieces, b_pieces = gather_pieces(shard)
    by_head = hold(
        cut_heads(query_rows[0], key_rows[0], value_rows[0]), *b_pieces
    )
    qkv = swap_ctx(by_head).reshape(SEQ, GW + 2 * DH)
    weights = (expert_gate, expert_in, expert_out)
    b_groups = terms(False, *project(b_pieces, *weights), expert_gate, expert_in)
    a_pieces[0] = hold(a_pieces[0], b_groups[0])
    a_groups = terms(True, *project(a_pieces, *weights), expert_gate, expert_in)
    settled = scatter_sums(a_groups, b_groups, qkv)
    part = swap_exp(settled.reshape(EXPERTS, 8, HALF)).reshape(TOK, HALF)
    probs, attended, q_sorted, kv_sorted = make_probs(span_order, qkv)
    grad_total, grad_cut = finish(stream[0], out_grad[0], gain, picks, part)
    grads = swap_ctx(grad_cut).reshape(SEQ, GW)
    result = attend(span_order, probs, attended, q_sorted, kv_sorted, grads)
    grad_query, grad_key, grad_value = place(
        swap_ctx(result.reshape(KVH, TOK, GW + 2 * DH))
    )
    return grad_total[None], grad_query[None], grad_key[None], grad_value[None]


def solution(mesh):
    rows = P("exp", "ctx", None)
    return jax.shard_map(
        body,
        mesh=mesh,
        in_specs=(
            rows,
            rows,
            rows,
            rows,
            rows,
            P("exp", "ctx"),
            rows,
            P(),
            P(),
            P("exp", None, "ctx"),
            P("exp", None, "ctx"),
            rows,
        ),
        out_specs=(rows, rows, rows, rows),
        check_vma=False,
    )
```

```python
import functools

import jax
import jax.numpy as jnp
from jax import lax
from jax.experimental import pallas as pl
from jax.experimental.pallas import tpu as pltpu
from jax.sharding import PartitionSpec as P

D = 5120
H = 40
KVH = 8
DH = 128
GROUP = H // KVH
EXPERTS = 16
CAP = 4
TOK = 128
SEQ = 1024
SPAN = 64
SPANS = SEQ // SPAN
FFD = 512
EPSILON = 1e-05
F32 = jnp.float32
BF16 = jnp.bfloat16
QB = 256
NQ = SEQ // QB
GW = GROUP * DH
HALF = D // 2
ROWS = 256
FIRST = 64
KB = 1280
TB = 2560
SHIFTS = (1, 3, 2)
FACTOR = DH ** (-0.5)


def nn(a, b):
    return lax.dot_general(a, b, (((1,), (0,)), ((), ())), preferred_element_type=F32)


def nt(a, b):
    return lax.dot_general(a, b, (((1,), (1,)), ((), ())), preferred_element_type=F32)


def tn(a, b):
    return lax.dot_general(a, b, (((0,), (0,)), ((), ())), preferred_element_type=F32)


def iota(shape, dim):
    return lax.broadcasted_iota(jnp.int32, shape, dim)


def params(mb=60):
    return pltpu.CompilerParams(vmem_limit_bytes=mb * 1024 * 1024)


def sds(shape, dtype=BF16):
    return jax.ShapeDtypeStruct(shape, dtype)


VM = pl.BlockSpec(memory_space=pltpu.VMEM)


def dispatch_kernel(stream, out_grad, weight, ids, gain, rows, picks):
    onehot = ids[...] == iota((TOK, 128), 1)
    onehot_f = onehot.astype(F32)
    lower = (iota((TOK, TOK), 1) < iota((TOK, TOK), 0)).astype(BF16)
    before = nn(lower, onehot_f.astype(BF16))
    rank = jnp.sum(before * onehot_f, axis=1, keepdims=True).astype(jnp.int32)
    lane = iota((TOK, 128), 1)
    target = ids[...] * 8 + rank
    kept = rank < CAP
    pick_n = ((lane == target) & kept).astype(BF16)
    pick_r = ((lane == target + CAP) & kept).astype(BF16)
    pick = jnp.concatenate([pick_n, pick_r], axis=0)
    picks[...] = pick
    total = jnp.zeros((TOK, 1), F32)
    for at in range(0, D, 640):
        part = stream[:, at:at + 640].astype(F32)
        total = total + jnp.sum(part * part, axis=1, keepdims=True)
    scale = lax.rsqrt(total / D + EPSILON)
    for at in range(0, D, 640):
        cols = slice(at, at + 640)
        normed = stream[:, cols].astype(F32) * scale * gain[:, cols]
        routed = out_grad[:, cols].astype(F32) * weight[...]
        both = jnp.concatenate([normed.astype(BF16), routed.astype(BF16)], axis=0)
        rows[:, cols] = tn(pick, both).astype(BF16)


def dispatch(stream, out_grad, weight, ids, gain):
    return pl.pallas_call(
        dispatch_kernel,
        out_shape=[sds((TOK, D)), sds((2 * TOK, 128))],
        in_specs=[VM] * 5,
        out_specs=[VM] * 2,
        compiler_params=params(24),
        name="dispatch",
    )(stream, out_grad, weight, ids, gain)


def sort_kernel(shard, *outs):
    out = iota((128, 128), 0)
    want = (out >> 6) * 64 + ((out >> 2) & 7) * 8 + ((out >> 5) & 1) * 4 + (out & 3)
    mover = (iota((128, 128), 1) == want).astype(BF16)
    for at in range(0, D, 1280):
        moved = nn(mover, shard[:, at:at + 1280]).astype(BF16)
        outs[0][:, at:at + 1280] = moved[:64]
        outs[1][:, at:at + 1280] = moved[64:]


def sort_rows(shard):
    return pl.pallas_call(
        sort_kernel,
        out_shape=[sds((64, D))] * 2,
        in_specs=[VM],
        out_specs=[VM] * 2,
        compiler_params=params(24),
        name="sort_rows",
    )(shard)


def project_kernel(n_pieces, *refs):
    pieces = refs[:n_pieces]
    w_gate, w_in, w_out, grad_gate, grad_up, x_at, r_at, gate, up, backed = refs[n_pieces:]
    step = pl.program_id(0)

    @pl.when(step == 0)
    def _():
        gate[...] = jnp.zeros_like(gate)
        up[...] = jnp.zeros_like(up)
        backed[...] = jnp.zeros_like(backed)

    at = 0
    for piece in pieces:
        for low in range(0, piece.shape[0], 64):
            x_at[at:at + 32, :] = piece[low:low + 32, :]
            r_at[at:at + 32, :] = piece[low + 32:low + 64, :]
            at += 32
    gate[...] += nn(x_at[...], w_gate[0])
    up[...] += nn(x_at[...], w_in[0])
    backed[...] += nt(r_at[...], w_out[0])

    @pl.when(step == pl.num_programs(0) - 1)
    def _():
        sig = jax.nn.sigmoid(gate[...])
        grad_gate[...] = (
            backed[...] * up[...] * sig * (1.0 + gate[...] * (1.0 - sig))
        ).astype(BF16)
        grad_up[...] = (backed[...] * gate[...] * sig).astype(BF16)


def project(pieces, w_gate, w_in, w_out):
    whole = pl.BlockSpec((ROWS, FFD), lambda i: (0, 0))
    in_specs = [pl.BlockSpec((p.shape[0], KB), lambda i: (0, i)) for p in pieces]
    in_specs += [
        pl.BlockSpec((1, KB, FFD), lambda i: (0, i, 0)),
        pl.BlockSpec((1, KB, FFD), lambda i: (0, i, 0)),
        pl.BlockSpec((1, FFD, KB), lambda i: (0, 0, i)),
    ]
    return pl.pallas_call(
        functools.partial(project_kernel, len(pieces)),
        grid=(D // KB,),
        out_shape=[sds((ROWS, FFD))] * 2,
        in_specs=in_specs,
        out_specs=[whole] * 2,
        scratch_shapes=[pltpu.VMEM((ROWS, KB), BF16)] * 2
        + [pltpu.VMEM((ROWS, FFD), F32)] * 3,
        compiler_params=params(60),
        cost_estimate=pl.CostEstimate(
            flops=6 * ROWS * D * FFD, bytes_accessed=28 * 1024 * 1024, transcendentals=0
        ),
        name="project",
    )(*pieces, w_gate, w_in, w_out)


def term_kernel(by_z, grad_gate, grad_up, w_gate, w_in, *outs):
    block = nt(grad_gate[...], w_gate[0]) + nt(grad_up[...], w_in[0])
    block = block.astype(BF16)
    for z in range(4):
        for side in range(2):
            rows = block[(2 * z + side) * 32:(2 * z + side + 1) * 32]
            if by_z:
                outs[z][side * 32:(side + 1) * 32, :] = rows
            else:
                outs[side][z * 32:(z + 1) * 32, :] = rows


def terms(by_z, grad_gate, grad_up, w_gate, w_in):
    whole = pl.BlockSpec(grad_gate.shape, lambda i: (0, 0))
    weight = pl.BlockSpec((1, TB, FFD), lambda i: (0, i, 0))
    sizes = (64,) * 4 if by_z else (128,) * 2
    return pl.pallas_call(
        functools.partial(term_kernel, by_z),
        grid=(D // TB,),
        out_shape=[sds((r, D)) for r in sizes],
        in_specs=[whole, whole, weight, weight],
        out_specs=[pl.BlockSpec((r, TB), lambda i: (0, i)) for r in sizes],
        compiler_params=params(60),
        cost_estimate=pl.CostEstimate(
            flops=4 * ROWS * D * FFD, bytes_accessed=14 * 1024 * 1024, transcendentals=0
        ),
        name="terms",
    )(grad_gate, grad_up, w_gate, w_in)


def settle_kernel(a_own, a_swap, b_own, b1, b3, b2, out):
    a = a_own[...] + a_swap[...].astype(F32)
    b = b_own[...] + b1[...].astype(F32) + b3[...].astype(F32) + b2[...].astype(F32)
    both = jnp.concatenate([a, b], axis=0).astype(BF16)
    stacked = jnp.concatenate([both[:, :HALF], both[:, HALF:]], axis=0)
    o = iota((128, 128), 0)
    want = ((o >> 2) & 1) * 64 + (o >> 3) * 4 + (o & 3)
    mover = (iota((128, 128), 1) == want).astype(BF16)
    out[...] = nn(mover, stacked).astype(BF16)


def settle(*args):
    return pl.pallas_call(
        settle_kernel,
        out_shape=sds((128, HALF)),
        in_specs=[VM] * 6,
        out_specs=VM,
        compiler_params=params(24),
        name="settle",
    )(*args)


def finish_kernel(stream, out_grad, gain, picks, part, grad, grad_cut, scaled):
    square = jnp.zeros((TOK, 1), F32)
    dots = jnp.zeros((TOK, 1), F32)
    for at in range(0, HALF, 640):
        got = nn(picks[...], part[:, at:at + 640])
        for half in range(2):
            cols = slice(half * HALF + at, half * HALF + at + 640)
            x = stream[:, cols].astype(F32)
            u = got[half * TOK:(half + 1) * TOK] * gain[:, cols]
            square = square + jnp.sum(x * x, axis=1, keepdims=True)
            dots = dots + jnp.sum(x * u, axis=1, keepdims=True)
            scaled[:, cols] = u
    r = lax.rsqrt(square / D + EPSILON)
    coef = dots * (r * r * r) / D
    for group in range(KVH):
        cols = slice(group * GW, (group + 1) * GW)
        x = stream[:, cols].astype(F32)
        total = out_grad[:, cols].astype(F32) + (scaled[:, cols] * r - x * coef)
        total = total.astype(BF16)
        grad[:, cols] = total
        grad_cut[group] = total


def finish(stream, out_grad, gain, picks, part):
    return pl.pallas_call(
        finish_kernel,
        out_shape=[sds((TOK, D)), sds((KVH, TOK, GW))],
        in_specs=[VM] * 5,
        out_specs=[VM] * 2,
        scratch_shapes=[pltpu.VMEM((TOK, D), F32)],
        compiler_params=params(24),
        name="finish",
    )(stream, out_grad, gain, picks, part)


def cut_kernel(q, k, v, out):
    for head in range(KVH):
        out[head, :, :GW] = q[:, head * GW:(head + 1) * GW]
        out[head, :, GW:GW + DH] = k[:, head * DH:(head + 1) * DH]
        out[head, :, GW + DH:] = v[:, head * DH:(head + 1) * DH]


def cut_heads(q, k, v):
    return pl.pallas_call(
        cut_kernel,
        out_shape=sds((KVH, TOK, GW + 2 * DH)),
        in_specs=[VM] * 3,
        out_specs=VM,
        compiler_params=params(),
        name="cut_heads",
    )(q, k, v)


def probs_kernel(order, rows, probs, attended, q_out, kv_out, q_at, kv_at, vt_at):
    head = pl.program_id(0)

    @pl.when(head == 0)
    def _():
        for s in range(SPANS):
            to = pl.ds(pl.multiple_of(order[s] * SPAN, SPAN), SPAN)
            block = rows[s * SPAN:(s + 1) * SPAN, :]
            for g in range(GROUP):
                q_at[g, to, :] = block[:, g * DH:(g + 1) * DH]
            kv_at[0, to, :] = block[:, GW:GW + DH]
            kv_at[1, to, :] = block[:, GW + DH:GW + 2 * DH]
        q_out[...] = q_at[...]
        kv_out[...] = kv_at[...]
        vt_at[...] = kv_at[1].T

    for i in range(NQ):
        n = QB * (i + 1)
        q = q_at[head, i * QB:n, :]
        scores = nt(kv_at[0, 0:n, :], q) * FACTOR
        visible = iota((n, QB), 0) <= iota((n, QB), 1) + i * QB
        scores = jnp.where(visible, scores, -1e30)
        peak = jnp.max(scores, axis=0, keepdims=True)
        weights = jnp.exp(scores - peak)
        weights = weights / jnp.sum(weights, axis=0, keepdims=True)
        weights_b = weights.astype(BF16)
        probs[0, i, 0:n, :] = weights_b
        attended[0, :, i * QB:n] = nn(vt_at[:, 0:n], weights_b)


def make_probs(order, rows):
    return pl.pallas_call(
        probs_kernel,
        grid_spec=pltpu.PrefetchScalarGridSpec(
            num_scalar_prefetch=1,
            grid=(GROUP,),
            in_specs=[pl.BlockSpec((SEQ, GW + 2 * DH), lambda h, o: (0, 0))],
            out_specs=[
                pl.BlockSpec((1, NQ, SEQ, QB), lambda h, o: (h, 0, 0, 0)),
                pl.BlockSpec((1, DH, SEQ), lambda h, o: (h, 0, 0)),
                pl.BlockSpec((GROUP, SEQ, DH), lambda h, o: (0, 0, 0)),
                pl.BlockSpec((2, SEQ, DH), lambda h, o: (0, 0, 0)),
            ],
            scratch_shapes=[
                pltpu.VMEM((GROUP, SEQ, DH), BF16),
                pltpu.VMEM((2, SEQ, DH), BF16),
                pltpu.VMEM((DH, SEQ), BF16),
            ],
        ),
        out_shape=[
            sds((GROUP, NQ, SEQ, QB)),
            sds((GROUP, DH, SEQ), F32),
            sds((GROUP, SEQ, DH)),
            sds((2, SEQ, DH)),
        ],
        compiler_params=params(),
        cost_estimate=pl.CostEstimate(
            flops=2 * GROUP * SEQ * SEQ * DH, bytes_accessed=14 * 1024 * 1024, transcendentals=GROUP * SEQ * SEQ
        ),
        name="probs",
    )(order, rows)


def attend_kernel(
    order, probs, attended, q, kv, grads, out, g_at, kt_at, dq_at, dk_at, dv_at
):
    head = pl.program_id(0)

    @pl.when(head == 0)
    def _():
        for s in range(SPANS):
            to = pl.ds(pl.multiple_of(order[s] * SPAN, SPAN), SPAN)
            block = grads[s * SPAN:(s + 1) * SPAN, :]
            for g in range(GROUP):
                g_at[g, to, :] = block[:, g * DH:(g + 1) * DH]
        kt_at[...] = kv[0].T
        dk_at[...] = jnp.zeros_like(dk_at)
        dv_at[...] = jnp.zeros_like(dv_at)

    g_t = g_at[head].T
    delta = jnp.sum(g_t.astype(F32) * attended[0], axis=0, keepdims=True)
    for i in range(NQ):
        n = QB * (i + 1)
        g_i = g_at[head, i * QB:n, :]
        q_i = q[head, i * QB:n, :]
        p_b = probs[0, i, 0:n, :]
        dp = nn(kv[1, 0:n, :], g_t[:, i * QB:n])
        ds = (p_b.astype(F32) * (dp - delta[:, i * QB:n])).astype(BF16)
        dv_at[0:n, :] += nn(p_b, g_i)
        dk_at[0:n, :] += nn(ds, q_i)
        dq_at[i * QB:n, :] = (nn(kt_at[:, 0:n], ds) * FACTOR).T.astype(BF16)
    for s in range(SPANS):
        at = pl.ds(pl.multiple_of(order[s] * SPAN, SPAN), SPAN)
        to = slice(s * SPAN, (s + 1) * SPAN)
        out[to, pl.ds(pl.multiple_of(head * DH, DH), DH)] = dq_at[at, :]

    @pl.when(head == GROUP - 1)
    def _():
        for s in range(SPANS):
            at = pl.ds(pl.multiple_of(order[s] * SPAN, SPAN), SPAN)
            to = slice(s * SPAN, (s + 1) * SPAN)
            out[to, GW:GW + DH] = (dk_at[at, :] * FACTOR).astype(BF16)
            out[to, GW + DH:GW + 2 * DH] = dv_at[at, :].astype(BF16)


def attend(order, probs, attended, q, kv, grads):
    return pl.pallas_call(
        attend_kernel,
        grid_spec=pltpu.PrefetchScalarGridSpec(
            num_scalar_prefetch=1,
            grid=(GROUP,),
            in_specs=[
                pl.BlockSpec((1, NQ, SEQ, QB), lambda h, o: (h, 0, 0, 0)),
                pl.BlockSpec((1, DH, SEQ), lambda h, o: (h, 0, 0)),
                pl.BlockSpec((GROUP, SEQ, DH), lambda h, o: (0, 0, 0)),
                pl.BlockSpec((2, SEQ, DH), lambda h, o: (0, 0, 0)),
                pl.BlockSpec((SEQ, GW), lambda h, o: (0, 0)),
            ],
            out_specs=pl.BlockSpec((SEQ, GW + 2 * DH), lambda h, o: (0, 0)),
            scratch_shapes=[
                pltpu.VMEM((GROUP, SEQ, DH), BF16),
                pltpu.VMEM((DH, SEQ), BF16),
                pltpu.VMEM((SEQ, DH), BF16),
                pltpu.VMEM((SEQ, DH), F32),
                pltpu.VMEM((SEQ, DH), F32),
            ],
        ),
        out_shape=sds((SEQ, GW + 2 * DH)),
        compiler_params=params(),
        cost_estimate=pl.CostEstimate(
            flops=8 * GROUP * SEQ * SEQ * DH, bytes_accessed=16 * 1024 * 1024, transcendentals=0
        ),
        name="attend",
    )(order, probs, attended, q, kv, grads)


def hold(x, *others):
    anywhere = pl.BlockSpec(memory_space=pl.ANY)
    return pl.pallas_call(
        lambda *refs: None,
        out_shape=sds(x.shape, x.dtype),
        in_specs=[anywhere] * (1 + len(others)),
        out_specs=anywhere,
        input_output_aliases={0: 0},
        name="hold",
    )(x, *others)


def place_kernel(block, dq, dk, dv):
    dq[...] = block[0, :, :GW]
    dk[...] = block[0, :, GW:GW + DH]
    dv[...] = block[0, :, GW + DH:]


def place(blocks):
    return pl.pallas_call(
        place_kernel,
        grid=(KVH,),
        out_shape=[sds((TOK, D)), sds((TOK, KVH * DH)), sds((TOK, KVH * DH))],
        in_specs=[pl.BlockSpec((1, TOK, GW + 2 * DH), lambda i: (i, 0, 0))],
        out_specs=[
            pl.BlockSpec((TOK, GW), lambda i: (0, i)),
            pl.BlockSpec((TOK, DH), lambda i: (0, i)),
            pl.BlockSpec((TOK, DH), lambda i: (0, i)),
        ],
        compiler_params=params(24),
        name="place",
    )(blocks)


def along_z(x, shift):
    pairs = [(c, ((c // 2 + shift) % 4) * 2 + c % 2) for c in range(8)]
    return lax.ppermute(x, "ctx", pairs)


def across_x(x):
    return lax.ppermute(x, "ctx", [(c, c ^ 1) for c in range(8)])


def gather_pieces(shard):
    a, b = sort_rows(shard)
    a_x = across_x(a)
    b_z = [along_z(b, k) for k in SHIFTS]
    a_both = jnp.concatenate([a, a_x], axis=0)
    a_z = [along_z(a_both, k) for k in SHIFTS]
    rests = []
    for p in [b] + b_z:
        rests += [p, across_x(p)]
    return [a_both] + a_z, rests


def scatter_sums(a_groups, b_groups, tie):
    a_own, (b_own, b_far) = a_groups[0], b_groups
    b_got = across_x(hold(b_far, tie))
    a_got = [along_z(g, -k) for g, k in zip(a_groups[1:], SHIFTS)]
    b_sum = b_own.astype(F32) + b_got.astype(F32)
    b_low = b_sum.astype(BF16)
    b_back = [
        along_z(b_low[32 * (at + 1):32 * (at + 2)], -k) for at, k in enumerate(SHIFTS)
    ]
    a_sum = a_own.astype(F32)
    for got in a_got:
        a_sum = a_sum + got.astype(F32)
    a_swap = across_x(a_sum[32:].astype(BF16))
    return settle(a_sum[:32], a_swap, b_sum[:32], *b_back)


def swap_exp(x):
    return lax.all_to_all(x, "exp", split_axis=0, concat_axis=0, tiled=True)


def swap_ctx(x):
    return lax.all_to_all(x, "ctx", split_axis=0, concat_axis=0, tiled=True)


def body(
    query_rows,
    key_rows,
    value_rows,
    stream,
    out_grad,
    route_weight,
    expert_ids,
    span_order,
    norm_gain,
    expert_gate,
    expert_in,
    expert_out,
):
    gain = norm_gain.reshape(1, D)
    outgoing, picks = dispatch(
        stream[0], out_grad[0], route_weight.reshape(TOK, 1), expert_ids[0], gain
    )
    shard = swap_exp(outgoing.reshape(EXPERTS, 8, D)).reshape(TOK, D)
    a_pieces, b_pieces = gather_pieces(shard)
    by_head = hold(
        cut_heads(query_rows[0], key_rows[0], value_rows[0]), *b_pieces
    )
    qkv = swap_ctx(by_head).reshape(SEQ, GW + 2 * DH)
    weights = (expert_gate, expert_in, expert_out)
    b_groups = terms(False, *project(b_pieces, *weights), expert_gate, expert_in)
    a_pieces[0] = hold(a_pieces[0], b_groups[0])
    a_groups = terms(True, *project(a_pieces, *weights), expert_gate, expert_in)
    settled = scatter_sums(a_groups, b_groups, qkv)
    part = swap_exp(settled.reshape(EXPERTS, 8, HALF)).reshape(TOK, HALF)
    probs, attended, q_sorted, kv_sorted = make_probs(span_order, qkv)
    grad_total, grad_cut = finish(stream[0], out_grad[0], gain, picks, part)
    grads = swap_ctx(grad_cut).reshape(SEQ, GW)
    result = attend(span_order, probs, attended, q_sorted, kv_sorted, grads)
    grad_query, grad_key, grad_value = place(
        swap_ctx(result.reshape(KVH, TOK, GW + 2 * DH))
    )
    return grad_total[None], grad_query[None], grad_key[None], grad_value[None]


def solution(mesh):
    rows = P("exp", "ctx", None)
    return jax.shard_map(
        body,
        mesh=mesh,
        in_specs=(
            rows,
            rows,
            rows,
            rows,
            rows,
            P("exp", "ctx"),
            rows,
            P(),
            P(),
            P("exp", None, "ctx"),
            P("exp", None, "ctx"),
            rows,
        ),
        out_specs=(rows, rows, rows, rows),
        check_vma=False,
    )
```

```python
import functools

import jax
import jax.numpy as jnp
from jax import lax
from jax.experimental import pallas as pl
from jax.experimental.pallas import tpu as pltpu
from jax.sharding import PartitionSpec as P

D = 5120
H = 40
KVH = 8
DH = 128
GROUP = H // KVH
EXPERTS = 16
CAP = 4
TOK = 128
SEQ = 1024
SPAN = 64
SPANS = SEQ // SPAN
FFD = 512
EPSILON = 1e-05
F32 = jnp.float32
BF16 = jnp.bfloat16
QB = 256
NQ = SEQ // QB
GW = GROUP * DH
HALF = D // 2
ROWS = 256
FIRST = 64
KB = 1280
TB = 2560
SHIFTS = (1, 3, 2)
FACTOR = DH ** (-0.5)


def nn(a, b):
    return lax.dot_general(a, b, (((1,), (0,)), ((), ())), preferred_element_type=F32)


def nt(a, b):
    return lax.dot_general(a, b, (((1,), (1,)), ((), ())), preferred_element_type=F32)


def tn(a, b):
    return lax.dot_general(a, b, (((0,), (0,)), ((), ())), preferred_element_type=F32)


def iota(shape, dim):
    return lax.broadcasted_iota(jnp.int32, shape, dim)


def params(mb=60):
    return pltpu.CompilerParams(vmem_limit_bytes=mb * 1024 * 1024)


def sds(shape, dtype=BF16):
    return jax.ShapeDtypeStruct(shape, dtype)


VM = pl.BlockSpec(memory_space=pltpu.VMEM)


def dispatch_kernel(stream, out_grad, weight, ids, gain, rows, picks):
    onehot = ids[...] == iota((TOK, 128), 1)
    onehot_f = onehot.astype(F32)
    lower = (iota((TOK, TOK), 1) < iota((TOK, TOK), 0)).astype(BF16)
    before = nn(lower, onehot_f.astype(BF16))
    rank = jnp.sum(before * onehot_f, axis=1, keepdims=True).astype(jnp.int32)
    lane = iota((TOK, 128), 1)
    target = ids[...] * 8 + rank
    kept = rank < CAP
    pick_n = ((lane == target) & kept).astype(BF16)
    pick_r = ((lane == target + CAP) & kept).astype(BF16)
    pick = jnp.concatenate([pick_n, pick_r], axis=0)
    picks[...] = pick
    total = jnp.zeros((TOK, 1), F32)
    for at in range(0, D, 640):
        part = stream[:, at:at + 640].astype(F32)
        total = total + jnp.sum(part * part, axis=1, keepdims=True)
    scale = lax.rsqrt(total / D + EPSILON)
    for at in range(0, D, 640):
        cols = slice(at, at + 640)
        normed = stream[:, cols].astype(F32) * scale * gain[:, cols]
        routed = out_grad[:, cols].astype(F32) * weight[...]
        both = jnp.concatenate([normed.astype(BF16), routed.astype(BF16)], axis=0)
        rows[:, cols] = tn(pick, both).astype(BF16)


def dispatch(stream, out_grad, weight, ids, gain):
    return pl.pallas_call(
        dispatch_kernel,
        out_shape=[sds((TOK, D)), sds((2 * TOK, 128))],
        in_specs=[VM] * 5,
        out_specs=[VM] * 2,
        compiler_params=params(24),
        name="dispatch",
    )(stream, out_grad, weight, ids, gain)


def sort_kernel(shard, *outs):
    out = iota((128, 128), 0)
    want = (out >> 6) * 64 + ((out >> 2) & 7) * 8 + ((out >> 5) & 1) * 4 + (out & 3)
    mover = (iota((128, 128), 1) == want).astype(BF16)
    for at in range(0, D, 1280):
        moved = nn(mover, shard[:, at:at + 1280]).astype(BF16)
        outs[0][:, at:at + 1280] = moved[:64]
        outs[1][:, at:at + 1280] = moved[64:]


def sort_rows(shard):
    return pl.pallas_call(
        sort_kernel,
        out_shape=[sds((64, D))] * 2,
        in_specs=[VM],
        out_specs=[VM] * 2,
        compiler_params=params(24),
        name="sort_rows",
    )(shard)


def project_kernel(n_pieces, *refs):
    pieces = refs[:n_pieces]
    w_gate, w_in, w_out, grad_gate, grad_up, x_at, r_at, gate, up, backed = refs[n_pieces:]
    step = pl.program_id(0)

    @pl.when(step == 0)
    def _():
        gate[...] = jnp.zeros_like(gate)
        up[...] = jnp.zeros_like(up)
        backed[...] = jnp.zeros_like(backed)

    at = 0
    for piece in pieces:
        for low in range(0, piece.shape[0], 64):
            x_at[at:at + 32, :] = piece[low:low + 32, :]
            r_at[at:at + 32, :] = piece[low + 32:low + 64, :]
            at += 32
    gate[...] += nn(x_at[...], w_gate[0])
    up[...] += nn(x_at[...], w_in[0])
    backed[...] += nt(r_at[...], w_out[0])

    @pl.when(step == pl.num_programs(0) - 1)
    def _():
        sig = jax.nn.sigmoid(gate[...])
        grad_gate[...] = (
            backed[...] * up[...] * sig * (1.0 + gate[...] * (1.0 - sig))
        ).astype(BF16)
        grad_up[...] = (backed[...] * gate[...] * sig).astype(BF16)


def project(pieces, w_gate, w_in, w_out):
    whole = pl.BlockSpec((ROWS, FFD), lambda i: (0, 0))
    in_specs = [pl.BlockSpec((p.shape[0], KB), lambda i: (0, i)) for p in pieces]
    in_specs += [
        pl.BlockSpec((1, KB, FFD), lambda i: (0, i, 0)),
        pl.BlockSpec((1, KB, FFD), lambda i: (0, i, 0)),
        pl.BlockSpec((1, FFD, KB), lambda i: (0, 0, i)),
    ]
    return pl.pallas_call(
        functools.partial(project_kernel, len(pieces)),
        grid=(D // KB,),
        out_shape=[sds((ROWS, FFD))] * 2,
        in_specs=in_specs,
        out_specs=[whole] * 2,
        scratch_shapes=[pltpu.VMEM((ROWS, KB), BF16)] * 2
        + [pltpu.VMEM((ROWS, FFD), F32)] * 3,
        compiler_params=params(60),
        cost_estimate=pl.CostEstimate(
            flops=6 * ROWS * D * FFD, bytes_accessed=28 * 1024 * 1024, transcendentals=0
        ),
        name="project",
    )(*pieces, w_gate, w_in, w_out)


def term_kernel(by_z, grad_gate, grad_up, w_gate, w_in, *outs):
    block = nt(grad_gate[...], w_gate[0]) + nt(grad_up[...], w_in[0])
    block = block.astype(BF16)
    for z in range(4):
        for side in range(2):
            rows = block[(2 * z + side) * 32:(2 * z + side + 1) * 32]
            if by_z:
                outs[z][side * 32:(side + 1) * 32, :] = rows
            else:
                outs[side][z * 32:(z + 1) * 32, :] = rows


def terms(by_z, grad_gate, grad_up, w_gate, w_in):
    whole = pl.BlockSpec(grad_gate.shape, lambda i: (0, 0))
    weight = pl.BlockSpec((1, TB, FFD), lambda i: (0, i, 0))
    sizes = (64,) * 4 if by_z else (128,) * 2
    return pl.pallas_call(
        functools.partial(term_kernel, by_z),
        grid=(D // TB,),
        out_shape=[sds((r, D)) for r in sizes],
        in_specs=[whole, whole, weight, weight],
        out_specs=[pl.BlockSpec((r, TB), lambda i: (0, i)) for r in sizes],
        compiler_params=params(60),
        cost_estimate=pl.CostEstimate(
            flops=4 * ROWS * D * FFD, bytes_accessed=14 * 1024 * 1024, transcendentals=0
        ),
        name="terms",
    )(grad_gate, grad_up, w_gate, w_in)


def settle_kernel(a_own, a_swap, b_own, b1, b3, b2, out):
    a = a_own[...] + a_swap[...].astype(F32)
    b = b_own[...] + b1[...].astype(F32) + b3[...].astype(F32) + b2[...].astype(F32)
    both = jnp.concatenate([a, b], axis=0).astype(BF16)
    stacked = jnp.concatenate([both[:, :HALF], both[:, HALF:]], axis=0)
    o = iota((128, 128), 0)
    want = ((o >> 2) & 1) * 64 + (o >> 3) * 4 + (o & 3)
    mover = (iota((128, 128), 1) == want).astype(BF16)
    out[...] = nn(mover, stacked).astype(BF16)


def settle(*args):
    return pl.pallas_call(
        settle_kernel,
        out_shape=sds((128, HALF)),
        in_specs=[VM] * 6,
        out_specs=VM,
        compiler_params=params(24),
        name="settle",
    )(*args)


def finish_kernel(stream, out_grad, gain, picks, part, grad, grad_cut, scaled):
    square = jnp.zeros((TOK, 1), F32)
    dots = jnp.zeros((TOK, 1), F32)
    for at in range(0, HALF, 640):
        got = nn(picks[...], part[:, at:at + 640])
        for half in range(2):
            cols = slice(half * HALF + at, half * HALF + at + 640)
            x = stream[:, cols].astype(F32)
            u = got[half * TOK:(half + 1) * TOK] * gain[:, cols]
            square = square + jnp.sum(x * x, axis=1, keepdims=True)
            dots = dots + jnp.sum(x * u, axis=1, keepdims=True)
            scaled[:, cols] = u
    r = lax.rsqrt(square / D + EPSILON)
    coef = dots * (r * r * r) / D
    for group in range(KVH):
        cols = slice(group * GW, (group + 1) * GW)
        x = stream[:, cols].astype(F32)
        total = out_grad[:, cols].astype(F32) + (scaled[:, cols] * r - x * coef)
        total = total.astype(BF16)
        grad[:, cols] = total
        grad_cut[group] = total


def finish(stream, out_grad, gain, picks, part):
    return pl.pallas_call(
        finish_kernel,
        out_shape=[sds((TOK, D)), sds((KVH, TOK, GW))],
        in_specs=[VM] * 5,
        out_specs=[VM] * 2,
        scratch_shapes=[pltpu.VMEM((TOK, D), F32)],
        compiler_params=params(24),
        name="finish",
    )(stream, out_grad, gain, picks, part)


def cut_kernel(q, k, v, out):
    for head in range(KVH):
        out[head, :, :GW] = q[:, head * GW:(head + 1) * GW]
        out[head, :, GW:GW + DH] = k[:, head * DH:(head + 1) * DH]
        out[head, :, GW + DH:] = v[:, head * DH:(head + 1) * DH]


def cut_heads(q, k, v):
    return pl.pallas_call(
        cut_kernel,
        out_shape=sds((KVH, TOK, GW + 2 * DH)),
        in_specs=[VM] * 3,
        out_specs=VM,
        compiler_params=params(),
        name="cut_heads",
    )(q, k, v)


def probs_kernel(order, rows, probs, attended, q_out, kv_out, q_at, kv_at, vt_at):
    head = pl.program_id(0)

    @pl.when(head == 0)
    def _():
        for s in range(SPANS):
            to = pl.ds(pl.multiple_of(order[s] * SPAN, SPAN), SPAN)
            block = rows[s * SPAN:(s + 1) * SPAN, :]
            for g in range(GROUP):
                q_at[g, to, :] = block[:, g * DH:(g + 1) * DH]
            kv_at[0, to, :] = block[:, GW:GW + DH]
            kv_at[1, to, :] = block[:, GW + DH:GW + 2 * DH]
        q_out[...] = q_at[...]
        kv_out[...] = kv_at[...]
        vt_at[...] = kv_at[1].T

    for i in range(NQ):
        n = QB * (i + 1)
        q = q_at[head, i * QB:n, :]
        scores = nt(kv_at[0, 0:n, :], q) * FACTOR
        visible = iota((n, QB), 0) <= iota((n, QB), 1) + i * QB
        scores = jnp.where(visible, scores, -1e30)
        peak = jnp.max(scores, axis=0, keepdims=True)
        weights = jnp.exp(scores - peak)
        weights = weights / jnp.sum(weights, axis=0, keepdims=True)
        weights_b = weights.astype(BF16)
        probs[0, i, 0:n, :] = weights_b
        attended[0, :, i * QB:n] = nn(vt_at[:, 0:n], weights_b)


def make_probs(order, rows):
    return pl.pallas_call(
        probs_kernel,
        grid_spec=pltpu.PrefetchScalarGridSpec(
            num_scalar_prefetch=1,
            grid=(GROUP,),
            in_specs=[pl.BlockSpec((SEQ, GW + 2 * DH), lambda h, o: (0, 0))],
            out_specs=[
                pl.BlockSpec((1, NQ, SEQ, QB), lambda h, o: (h, 0, 0, 0)),
                pl.BlockSpec((1, DH, SEQ), lambda h, o: (h, 0, 0)),
                pl.BlockSpec((GROUP, SEQ, DH), lambda h, o: (0, 0, 0)),
                pl.BlockSpec((2, SEQ, DH), lambda h, o: (0, 0, 0)),
            ],
            scratch_shapes=[
                pltpu.VMEM((GROUP, SEQ, DH), BF16),
                pltpu.VMEM((2, SEQ, DH), BF16),
                pltpu.VMEM((DH, SEQ), BF16),
            ],
        ),
        out_shape=[
            sds((GROUP, NQ, SEQ, QB)),
            sds((GROUP, DH, SEQ), F32),
            sds((GROUP, SEQ, DH)),
            sds((2, SEQ, DH)),
        ],
        compiler_params=params(),
        cost_estimate=pl.CostEstimate(
            flops=2 * GROUP * SEQ * SEQ * DH, bytes_accessed=14 * 1024 * 1024, transcendentals=GROUP * SEQ * SEQ
        ),
        name="probs",
    )(order, rows)


def attend_kernel(
    order, probs, attended, q, kv, grads, out, g_at, kt_at, dq_at, dk_at, dv_at
):
    head = pl.program_id(0)

    @pl.when(head == 0)
    def _():
        for s in range(SPANS):
            to = pl.ds(pl.multiple_of(order[s] * SPAN, SPAN), SPAN)
            block = grads[s * SPAN:(s + 1) * SPAN, :]
            for g in range(GROUP):
                g_at[g, to, :] = block[:, g * DH:(g + 1) * DH]
        kt_at[...] = kv[0].T
        dk_at[...] = jnp.zeros_like(dk_at)
        dv_at[...] = jnp.zeros_like(dv_at)

    g_t = g_at[head].T
    delta = jnp.sum(g_t.astype(F32) * attended[0], axis=0, keepdims=True)
    for i in range(NQ):
        n = QB * (i + 1)
        g_i = g_at[head, i * QB:n, :]
        q_i = q[head, i * QB:n, :]
        p_b = probs[0, i, 0:n, :]
        dp = nn(kv[1, 0:n, :], g_t[:, i * QB:n])
        ds = (p_b.astype(F32) * (dp - delta[:, i * QB:n])).astype(BF16)
        dv_at[0:n, :] += nn(p_b, g_i)
        dk_at[0:n, :] += nn(ds, q_i)
        dq_at[i * QB:n, :] = (nn(kt_at[:, 0:n], ds) * FACTOR).T.astype(BF16)
    for s in range(SPANS):
        at = pl.ds(pl.multiple_of(order[s] * SPAN, SPAN), SPAN)
        to = slice(s * SPAN, (s + 1) * SPAN)
        out[to, pl.ds(pl.multiple_of(head * DH, DH), DH)] = dq_at[at, :]

    @pl.when(head == GROUP - 1)
    def _():
        for s in range(SPANS):
            at = pl.ds(pl.multiple_of(order[s] * SPAN, SPAN), SPAN)
            to = slice(s * SPAN, (s + 1) * SPAN)
            out[to, GW:GW + DH] = (dk_at[at, :] * FACTOR).astype(BF16)
            out[to, GW + DH:GW + 2 * DH] = dv_at[at, :].astype(BF16)


def attend(order, probs, attended, q, kv, grads):
    return pl.pallas_call(
        attend_kernel,
        grid_spec=pltpu.PrefetchScalarGridSpec(
            num_scalar_prefetch=1,
            grid=(GROUP,),
            in_specs=[
                pl.BlockSpec((1, NQ, SEQ, QB), lambda h, o: (h, 0, 0, 0)),
                pl.BlockSpec((1, DH, SEQ), lambda h, o: (h, 0, 0)),
                pl.BlockSpec((GROUP, SEQ, DH), lambda h, o: (0, 0, 0)),
                pl.BlockSpec((2, SEQ, DH), lambda h, o: (0, 0, 0)),
                pl.BlockSpec((SEQ, GW), lambda h, o: (0, 0)),
            ],
            out_specs=pl.BlockSpec((SEQ, GW + 2 * DH), lambda h, o: (0, 0)),
            scratch_shapes=[
                pltpu.VMEM((GROUP, SEQ, DH), BF16),
                pltpu.VMEM((DH, SEQ), BF16),
                pltpu.VMEM((SEQ, DH), BF16),
                pltpu.VMEM((SEQ, DH), F32),
                pltpu.VMEM((SEQ, DH), F32),
            ],
        ),
        out_shape=sds((SEQ, GW + 2 * DH)),
        compiler_params=params(),
        cost_estimate=pl.CostEstimate(
            flops=8 * GROUP * SEQ * SEQ * DH, bytes_accessed=16 * 1024 * 1024, transcendentals=0
        ),
        name="attend",
    )(order, probs, attended, q, kv, grads)


def hold(x, *others):
    anywhere = pl.BlockSpec(memory_space=pl.ANY)
    return pl.pallas_call(
        lambda *refs: None,
        out_shape=sds(x.shape, x.dtype),
        in_specs=[anywhere] * (1 + len(others)),
        out_specs=anywhere,
        input_output_aliases={0: 0},
        name="hold",
    )(x, *others)


def place_kernel(block, dq, dk, dv):
    for k in range(2):
        dq[:, k * GW:(k + 1) * GW] = block[k, :, :GW]
        dk[:, k * DH:(k + 1) * DH] = block[k, :, GW:GW + DH]
        dv[:, k * DH:(k + 1) * DH] = block[k, :, GW + DH:]


def place(blocks):
    return pl.pallas_call(
        place_kernel,
        grid=(KVH // 2,),
        out_shape=[sds((TOK, D)), sds((TOK, KVH * DH)), sds((TOK, KVH * DH))],
        in_specs=[pl.BlockSpec((2, TOK, GW + 2 * DH), lambda i: (i, 0, 0))],
        out_specs=[
            pl.BlockSpec((TOK, 2 * GW), lambda i: (0, i)),
            pl.BlockSpec((TOK, 2 * DH), lambda i: (0, i)),
            pl.BlockSpec((TOK, 2 * DH), lambda i: (0, i)),
        ],
        compiler_params=params(24),
        name="place",
    )(blocks)


def along_z(x, shift):
    pairs = [(c, ((c // 2 + shift) % 4) * 2 + c % 2) for c in range(8)]
    return lax.ppermute(x, "ctx", pairs)


def across_x(x):
    return lax.ppermute(x, "ctx", [(c, c ^ 1) for c in range(8)])


def gather_pieces(shard):
    a, b = sort_rows(shard)
    a_x = across_x(a)
    b_z = [along_z(b, k) for k in SHIFTS]
    a_both = jnp.concatenate([a, a_x], axis=0)
    a_z = [along_z(a_both, k) for k in SHIFTS]
    rests = []
    for p in [b] + b_z:
        rests += [p, across_x(p)]
    return [a_both] + a_z, rests


def scatter_sums(a_groups, b_groups, tie):
    a_own, (b_own, b_far) = a_groups[0], b_groups
    b_got = across_x(hold(b_far, tie))
    a_got = [along_z(g, -k) for g, k in zip(a_groups[1:], SHIFTS)]
    b_sum = b_own.astype(F32) + b_got.astype(F32)
    b_low = b_sum.astype(BF16)
    b_back = [
        along_z(b_low[32 * (at + 1):32 * (at + 2)], -k) for at, k in enumerate(SHIFTS)
    ]
    a_sum = a_own.astype(F32)
    for got in a_got:
        a_sum = a_sum + got.astype(F32)
    a_swap = across_x(a_sum[32:].astype(BF16))
    return settle(a_sum[:32], a_swap, b_sum[:32], *b_back)


def swap_exp(x):
    return lax.all_to_all(x, "exp", split_axis=0, concat_axis=0, tiled=True)


def swap_ctx(x):
    return lax.all_to_all(x, "ctx", split_axis=0, concat_axis=0, tiled=True)


def body(
    query_rows,
    key_rows,
    value_rows,
    stream,
    out_grad,
    route_weight,
    expert_ids,
    span_order,
    norm_gain,
    expert_gate,
    expert_in,
    expert_out,
):
    gain = norm_gain.reshape(1, D)
    outgoing, picks = dispatch(
        stream[0], out_grad[0], route_weight.reshape(TOK, 1), expert_ids[0], gain
    )
    shard = swap_exp(outgoing.reshape(EXPERTS, 8, D)).reshape(TOK, D)
    a_pieces, b_pieces = gather_pieces(shard)
    by_head = hold(
        cut_heads(query_rows[0], key_rows[0], value_rows[0]), *b_pieces
    )
    qkv = swap_ctx(by_head).reshape(SEQ, GW + 2 * DH)
    weights = (expert_gate, expert_in, expert_out)
    b_groups = terms(False, *project(b_pieces, *weights), expert_gate, expert_in)
    a_pieces[0] = hold(a_pieces[0], b_groups[0])
    a_groups = terms(True, *project(a_pieces, *weights), expert_gate, expert_in)
    settled = scatter_sums(a_groups, b_groups, qkv)
    part = swap_exp(settled.reshape(EXPERTS, 8, HALF)).reshape(TOK, HALF)
    probs, attended, q_sorted, kv_sorted = make_probs(span_order, qkv)
    grad_total, grad_cut = finish(stream[0], out_grad[0], gain, picks, part)
    grads = swap_ctx(grad_cut).reshape(SEQ, GW)
    result = attend(span_order, probs, attended, q_sorted, kv_sorted, grads)
    grad_query, grad_key, grad_value = place(
        swap_ctx(result.reshape(KVH, TOK, GW + 2 * DH))
    )
    return grad_total[None], grad_query[None], grad_key[None], grad_value[None]


def solution(mesh):
    rows = P("exp", "ctx", None)
    return jax.shard_map(
        body,
        mesh=mesh,
        in_specs=(
            rows,
            rows,
            rows,
            rows,
            rows,
            P("exp", "ctx"),
            rows,
            P(),
            P(),
            P("exp", None, "ctx"),
            P("exp", None, "ctx"),
            rows,
        ),
        out_specs=(rows, rows, rows, rows),
        check_vma=False,
    )
```
